512 devices in a mesh: rows: 128 (over z, x, core), tower: 4 (over y).
Axes of the slice: x: 4, y: 4, z: 16, core: 2. Of those that a mesh axis runs over, the one named last changes fastest.
Arguments:
- pool_img: bfloat16 [65536, 1024], P('rows'), may hold values from -6 to 6
- pool_txt: bfloat16 [65536, 1024], P('rows'), may hold values from -6 to 6
- w_img: bfloat16 [1024, 512], P(None, 'tower'), may hold values from -1 to 1
- w_txt: bfloat16 [1024, 512], P(None, 'tower'), may hold values from -1 to 1
- logit_scale: float32 [1], replicated, may hold values from 16 to 40
- logit_bias: float32 [1], replicated, may hold values from -10 to -6
- loss_scale: float32 [1], replicated, may hold values from 256 to 1024
- select: int32 [32768], P('rows'), may hold values from 0 to 511, as said below
- counts: int32 [128], P('rows'), may hold values from 0 to 256, as said below
Outputs:
- grad_w_img: float32 [1024, 512], P('rows', 'tower')
- grad_w_txt: float32 [1024, 512], P('rows', 'tower')
The draws below stay inside these ranges and needn't reach their ends.
Inputs may be any that keep to these rules, and one draw needn't show every extreme that they name: `select`: each device's list names distinct rows of its own 512 super-batch rows. The counts of all devices sum to 16384; some device's count is 256.
All inputs are finite; a program needn't handle non-finite values.
Results may differ from the reference program's by a relative error of at most 0.0013.
Values may be sent and summed in bfloat16 or wider, within the bound.
A program may use at most 64 MiB of HBM per device.

```python
import math
import jax
import jax.numpy as jnp
from jax import lax

D = 1024
E = 512
POOL_DEV = 512
LRN = 128
SEL_MAX = 256
POOL = 65536
N_ROWS = 128


def draw_counts(key, part):
    key = jax.random.fold_in(key, 11)
    keys = jax.random.split(key, 2)
    device_order = jax.random.permutation(keys[0], N_ROWS)
    position = jnp.argsort(device_order).astype(jnp.int32)
    pair_at = position // 2
    sign_at = 1 - 2 * (position % 2)
    swing = jax.random.randint(keys[1], (N_ROWS // 2,), -LRN, LRN + 1).astype(jnp.int32)
    swing = swing.at[0].set(LRN)
    return (LRN + sign_at * swing[pair_at]).astype(jnp.int32)


def draw_select(key, part):
    key = jax.random.fold_in(key, 7)
    keys = jax.random.split(key, N_ROWS)

    def one_list(list_key):
        return jax.random.permutation(list_key, POOL_DEV)[:SEL_MAX]
    return jax.vmap(one_list)(keys).reshape(-1).astype(jnp.int32)


def pair_base(key):
    plan_key = jax.random.fold_in(key, 31)
    keys = jax.random.split(plan_key, 4)
    groups = max(LRN * N_ROWS // 32, 2)
    centres = jax.random.normal(keys[0], (groups, D), jnp.float32)
    member = jax.random.randint(keys[1], (POOL,), 0, groups).astype(jnp.int32)
    spread = jax.random.normal(keys[2], (POOL, D), jnp.float32)
    strength = jax.random.uniform(keys[3], (POOL, 1), jnp.float32, 0.05, 0.95)
    common = jnp.sqrt(0.8) * jnp.take(centres, member, axis=0) + jnp.sqrt(0.2) * spread
    return (common, strength)


def pair_features(common, strength, jitter):
    blended = jnp.sqrt(strength) * common + jnp.sqrt(1.0 - strength) * jitter
    return jnp.clip(blended, -6.0, 6.0).astype(jnp.bfloat16)


def draw_pool_img(key, part):
    common, strength = pair_base(key)
    key = jax.random.fold_in(key, 41)
    keys = jax.random.split(key, 1)
    jitter = jax.random.normal(keys[0], (POOL, D), jnp.float32)
    return pair_features(common, strength, jitter)


def draw_pool_txt(key, part):
    common, strength = pair_base(key)
    key = jax.random.fold_in(key, 42)
    keys = jax.random.split(key, 1)
    jitter = jax.random.normal(keys[0], (POOL, D), jnp.float32)
    return pair_features(common, strength, jitter)


def shared_weight(key):
    plan_key = jax.random.fold_in(key, 51)
    return jax.random.normal(plan_key, (D, E), jnp.float32)


def finish_weight(shared, own_part):
    blended = (jnp.sqrt(0.85) * shared + jnp.sqrt(0.15) * own_part) * D ** (-0.5)
    return jnp.clip(blended, -1.0, 1.0).astype(jnp.bfloat16)


def draw_w_img(key, part):
    shared = shared_weight(key)
    key = jax.random.fold_in(key, 61)
    own_part = jax.random.normal(key, (D, E), jnp.float32)
    return finish_weight(shared, own_part)


def draw_w_txt(key, part):
    shared = shared_weight(key)
    key = jax.random.fold_in(key, 62)
    own_part = jax.random.normal(key, (D, E), jnp.float32)
    return finish_weight(shared, own_part)


def setup_inputs(seed: int = 0) -> dict:
    splits = jax.random.split(jax.random.key(seed), 10)
    pool_img = draw_pool_img(jax.random.fold_in(splits[9], 71), 0)
    pool_txt = draw_pool_txt(jax.random.fold_in(splits[9], 71), 0)
    w_img = draw_w_img(jax.random.fold_in(splits[9], 71), 0)
    w_txt = draw_w_txt(jax.random.fold_in(splits[9], 71), 0)
    logit_scale = jnp.clip(jnp.exp(jax.random.uniform(splits[4], (1,), jnp.float32, math.log(16.0), math.log(40.0))), 16.0, 40.0)
    logit_bias = jnp.clip(jax.random.uniform(splits[5], (1,), jnp.float32, -10.0, -6.0), -10.0, -6.0)
    loss_scale = jnp.clip(jnp.exp(jax.random.uniform(splits[6], (1,), jnp.float32, math.log(256.0), math.log(1024.0))), 256.0, 1024.0)
    select = draw_select(jax.random.fold_in(splits[9], 71), 0)
    counts = draw_counts(jax.random.fold_in(splits[9], 71), 0)
    return dict(pool_img=pool_img, pool_txt=pool_txt, w_img=w_img, w_txt=w_txt, logit_scale=logit_scale, logit_bias=logit_bias, loss_scale=loss_scale, select=select, counts=counts)


eps = 1e-06

def unit_rows(feats, weight):
    proj = jnp.dot(feats, weight, preferred_element_type=jnp.float32)
    norm_val = lax.rsqrt(lax.optimization_barrier(jnp.sum(proj * proj, axis=1)) + eps)
    return (proj * norm_val[:, None], norm_val)

def side_grad(rows_emb, cols_emb, temper_val, bias_val, total_pairs):
    blocks = rows_emb.reshape(N_ROWS, LRN, rows_emb.shape[1])
    starts = jnp.arange(N_ROWS, dtype=jnp.int32) * LRN
    col_ids = jnp.arange(total_pairs, dtype=jnp.int32)

    def block_grad(packed):
        block_emb, first_row = packed
        logits = temper_val * jnp.dot(block_emb, cols_emb.T, preferred_element_type=jnp.float32) + bias_val
        row_ids = first_row + jnp.arange(LRN, dtype=jnp.int32)
        labels = (row_ids[:, None] == col_ids[None, :]).astype(jnp.float32)
        weights = (jax.nn.sigmoid(logits) - labels).astype(jnp.bfloat16)
        return jnp.dot(weights, cols_emb, preferred_element_type=jnp.float32)
    return lax.map(block_grad, (blocks, starts)).reshape(total_pairs, rows_emb.shape[1])

def reference(pool_img, pool_txt, w_img, w_txt, logit_scale, logit_bias, loss_scale, select, counts):
    total_pairs = LRN * N_ROWS
    list_len = SEL_MAX
    picks = select.reshape(N_ROWS, list_len) + (jnp.arange(N_ROWS, dtype=jnp.int32) * POOL_DEV)[:, None]
    picks = picks.reshape(-1).astype(jnp.int32)
    is_live = (jnp.arange(list_len, dtype=jnp.int32)[None, :] < counts[:, None]).reshape(-1)
    feats_img = pool_img[picks]
    feats_txt = pool_txt[picks]
    unit_img, norm_img = unit_rows(feats_img, w_img)
    unit_txt, norm_txt = unit_rows(feats_txt, w_txt)
    live_rank = jnp.cumsum(is_live.astype(jnp.int32)) - 1
    target_at = jnp.where(is_live, live_rank, total_pairs).astype(jnp.int32)
    slot_ids = jnp.arange(N_ROWS * list_len, dtype=jnp.int32)
    live_order = jnp.zeros((total_pairs,), jnp.int32).at[target_at].set(slot_ids, mode='drop')
    emb_img = unit_img.astype(jnp.bfloat16)[live_order]
    emb_txt = unit_txt.astype(jnp.bfloat16)[live_order]
    temper_val = logit_scale[0]
    bias_val = logit_bias[0]
    factor = loss_scale[0] * temper_val / total_pairs
    grad_emb_img = factor * side_grad(emb_img, emb_txt, temper_val, bias_val, total_pairs)
    grad_emb_txt = factor * side_grad(emb_txt, emb_img, temper_val, bias_val, total_pairs)
    slots_shape = (N_ROWS * list_len, unit_img.shape[1])
    grad_unit_img = jnp.zeros(slots_shape, jnp.float32).at[live_order].set(grad_emb_img)
    grad_unit_txt = jnp.zeros(slots_shape, jnp.float32).at[live_order].set(grad_emb_txt)
    inner_img = lax.optimization_barrier(jnp.sum(unit_img * grad_unit_img, axis=1))
    inner_txt = lax.optimization_barrier(jnp.sum(unit_txt * grad_unit_txt, axis=1))
    grad_proj_img = (norm_img[:, None] * (grad_unit_img - unit_img * inner_img[:, None])).astype(jnp.bfloat16)
    grad_proj_txt = (norm_txt[:, None] * (grad_unit_txt - unit_txt * inner_txt[:, None])).astype(jnp.bfloat16)
    grad_w_img = jnp.dot(feats_img.T, grad_proj_img, preferred_element_type=jnp.float32)
    grad_w_txt = jnp.dot(feats_txt.T, grad_proj_txt, preferred_element_type=jnp.float32)
    return (grad_w_img, grad_w_txt)
```

```python
import functools

import jax
import jax.numpy as jnp
from jax import lax
from jax.experimental import pallas as pl
from jax.experimental.pallas import tpu as pltpu
from jax.sharding import PartitionSpec as P

bf16 = jnp.bfloat16
f32 = jnp.float32
eps = 1e-06

NX, NC = 4, 2
LRN = 128
GROUP, TILE = 4, 4
ZCH = 2


def dot(a, b, ca=1, cb=0):
    return lax.dot_general(a, b, (((ca,), (cb,)), ((), ())), preferred_element_type=f32)


def chip_order(nx, ny):
    ring = lambda d, n: min(d, n - d)
    places = [(dx, dy) for dx in range(nx) for dy in range(ny)]
    return sorted(places, key=lambda p: (ring(p[0], nx) + ring(p[1], ny), p))


def kernel(
    cfg,
    pool_img, pool_txt, w_img, w_txt, sel, cnt, temper, bias, loss_scale,
    out_img, out_txt,
    feats, proj, unit, norm, zbuf, pbuf, gimg, gtxt, rz_up, rz_dn, rcore, sbuf, rxy,
    gp, gpr, gw, gwc, gx, gxr, gz, gzr,
    y_sem, za_up, za_dn, xy_sem, cf_sem, zr_up, zr_dn, cr_sem, xr_sem, yb_sem,
    fc_sem, fx_sem, fz_sem,
):
    nz, ny, chips = cfg
    row, y = lax.axis_index("rows"), lax.axis_index("tower")
    c = row % NC
    x = row // NC % NX
    z = row // (NC * NX)
    half = nz // 2
    order = chip_order(NX, ny)
    groups, tiles = nz // GROUP, len(order) // TILE
    slots = unit.shape[2]
    emb_w = zbuf.shape[2]
    col_w = proj.shape[2]
    sends = []

    def at(dz=0, dx=0, dy=0, dc=0):
        r = ((z + dz + nz) % nz * NX + (x + dx + NX) % NX) * NC + (c + dc) % NC
        return (r, (y + dy + ny) % ny)

    def send(src, dst, sems, where):
        copy = pltpu.make_async_remote_copy(
            src_ref=src, dst_ref=dst, send_sem=sems.at[0], recv_sem=sems.at[1],
            device_id=where, device_id_type=pl.DeviceIdType.MESH,
        )
        copy.start()
        sends.append(copy)

    def arrived(ref, sems):
        pltpu.make_async_remote_copy(
            src_ref=ref, dst_ref=ref, send_sem=sems.at[0], recv_sem=sems.at[1],
            device_id=at(), device_id_type=pl.DeviceIdType.MESH,
        ).wait_recv()

    partners = [at(dx=dx, dy=dy) for dx, dy in order[1:]]
    partners += [at(dz=dz) for dz in range(1, nz)] + [at(dc=1)]
    barrier = pltpu.get_barrier_semaphore()
    for there in partners:
        pl.semaphore_signal(
            barrier, inc=1, device_id=there, device_id_type=pl.DeviceIdType.MESH
        )

    pool_rows = pool_img.shape[0]
    cols = lax.broadcasted_iota(jnp.int32, (sel.shape[0], pool_rows), 1)
    pick = jnp.where(sel[...] == cols, 1.0, 0.0).astype(bf16)
    for side, (pool, w) in enumerate(((pool_img, w_img), (pool_txt, w_txt))):
        feats[side] = dot(pick, pool[...]).astype(bf16)
        proj[side] = dot(feats[side], w[...])
    pl.semaphore_wait(barrier, len(partners))

    for dy in range(1, ny):
        yy = (y + dy) % ny
        send(
            proj.at[:, pl.ds(pl.multiple_of(yy * slots, slots), slots)],
            unit.at[y], y_sem.at[dy - 1], at(dy=dy),
        )
    unit[y] = proj[:, pl.ds(pl.multiple_of(y * slots, slots), slots)]
    for dy in range(1, ny):
        arrived(unit.at[(y - dy + ny) % ny], y_sem.at[dy - 1])
    slot_at = y * slots + lax.broadcasted_iota(jnp.int32, (slots, 1), 0)
    live = slot_at < cnt[0]
    for side in range(2):
        square = sum(
            jnp.sum(unit[k, side] * unit[k, side], axis=1, keepdims=True) for k in range(ny)
        )
        norm[side] = lax.rsqrt(square + eps)
        for k in range(ny):
            unit[k, side] = unit[k, side] * norm[side]
            emb = jnp.where(live, unit[k, side], 0.0).astype(bf16)
            if side == 0:
                zbuf[0, :, k * col_w:(k + 1) * col_w] = emb
            else:
                pbuf[0, 0, :, k * col_w:(k + 1) * col_w] = emb

    def spot(offset):
        return 2 * offset if offset >= 0 else -2 * offset - 1

    zrows = slots // ZCH

    def ring_send(s):
        for h in range(ZCH):
            rows = pl.ds(h * zrows, zrows)
            if s > 1:
                arrived(zbuf.at[spot(1 - s), rows], za_up.at[s - 2, h])
            if s <= half:
                send(zbuf.at[spot(1 - s), rows], zbuf.at[spot(-s), rows],
                     za_up.at[s - 1, h], at(dz=1))
            if 1 < s <= nz - half:
                arrived(zbuf.at[spot(s - 1), rows], za_dn.at[s - 2, h])
            if s < nz - half:
                send(zbuf.at[spot(s - 1), rows], zbuf.at[spot(s), rows],
                     za_dn.at[s - 1, h], at(dz=-1))

    def hand_over(t):
        for n in range(t * TILE, (t + 1) * TILE):
            if n:
                arrived(pbuf.at[n, 0], xy_sem.at[n - 1])
                send(pbuf.at[n, 0], pbuf.at[n, 1], cf_sem.at[n], at(dc=1))

    def tile_ready(t):
        for n in range(t * TILE, (t + 1) * TILE):
            arrived(pbuf.at[n, 1], cf_sem.at[n])

    def pair_tile(g, t):
        img = zbuf[g * GROUP:(g + 1) * GROUP].reshape(GROUP * slots, emb_w)
        txt = pbuf[t * TILE:(t + 1) * TILE].reshape(TILE * NC * slots, emb_w)
        logits = temper[0] * dot(img, txt, 1, 1) + bias[0]
        weights = 1.0 / (1.0 + jnp.exp(-logits))
        if g == 0 and t == 0:
            i = lax.broadcasted_iota(jnp.int32, logits.shape, 0)
            j = lax.broadcasted_iota(jnp.int32, logits.shape, 1)
            weights = jnp.where((i == j) & (i < slots), 0.0, weights)
        weights = weights.astype(bf16)
        to_img = dot(weights, txt).reshape(GROUP, slots, emb_w)
        to_txt = dot(weights, img, 0, 0).reshape(TILE, NC, slots, emb_w)
        at_img = slice(g * GROUP, (g + 1) * GROUP)
        at_txt = slice(t * TILE, (t + 1) * TILE)
        gimg[at_img] = to_img if (g, t) in first_img else gimg[at_img] + to_img
        gtxt[at_txt] = to_txt if (g, t) in first_txt else gtxt[at_txt] + to_txt

    phases = []
    for k in range(groups):
        if k < groups - 1:
            phases.append([(k, t) for t in range(k)] + [(g, k) for g in range(k + 1)])
        else:
            phases.append([(k, t) for t in range(tiles)]
                          + [(g, k) for g in range(k - 1, -1, -1)])
    flat = [p for phase in phases for p in phase]
    first_img = {next(p for p in flat if p[0] == g) for g in range(groups)}
    first_txt = {next(p for p in flat if p[1] == t) for t in range(tiles)}

    queue = []
    opened = 0
    for s in range(1, half + 2):
        ring_send(s)
        if s == 1:
            send(pbuf.at[0, 0], pbuf.at[0, 1], cf_sem.at[0], at(dc=1))
            for n, (dx, dy) in enumerate(order[1:]):
                send(pbuf.at[0, 0], pbuf.at[n + 1, 0], xy_sem.at[n], at(dx=dx, dy=dy))
        if (s - 1) * 2 >= (opened + 1) * GROUP:
            tile_ready(opened)
            queue += phases[opened]
            opened += 1
        if s <= half:
            for p in queue[:2]:
                pair_tile(*p)
            queue = queue[2:]
        if opened < tiles and s * 2 >= (opened + 1) * GROUP:
            hand_over(opened)
    early = [p for p in queue if p[0] < groups - 1 and p[1] < tiles - 1]
    last = [p for p in queue if p[0] == groups - 1]
    rest = [p for p in queue if p[0] < groups - 1 and p[1] == tiles - 1]
    for p in early + last:
        pair_tile(*p)

    def ring_sum(s):
        for h in range(ZCH):
            rows = pl.ds(h * zrows, zrows)
            if s <= half:
                k = spot(half + 1 - s) if s > 1 else spot(-half)
                if s > 1:
                    arrived(rz_up.at[s - 2, rows], zr_up.at[s - 2, h])
                    gimg[k, rows] = gimg[k, rows] + rz_up[s - 2, rows]
                send(gimg.at[k, rows], rz_up.at[s - 1, rows], zr_up.at[s - 1, h], at(dz=1))
            if s < nz - half:
                k = spot(s - (nz - half))
                if s > 1:
                    arrived(rz_dn.at[s - 2, rows], zr_dn.at[s - 2, h])
                    gimg[k, rows] = gimg[k, rows] + rz_dn[s - 2, rows]
                send(gimg.at[k, rows], rz_dn.at[s - 1, rows], zr_dn.at[s - 1, h], at(dz=-1))

    def core_send():
        for t in range(tiles):
            part = pl.ds(t * TILE, TILE)
            send(gtxt.at[part, 1], rcore.at[part], cr_sem.at[t], at(dc=1))

    def plane_send(t):
        part = pl.ds(t * TILE, TILE)
        arrived(rcore.at[part], cr_sem.at[t])
        for n in range(t * TILE, (t + 1) * TILE):
            both = gtxt[n, 0] + rcore[n]
            if n == 0:
                gtxt[0, 0] = both
            else:
                sbuf[n] = both.astype(sbuf.dtype)
                dx, dy = order[n]
                send(sbuf.at[n], rxy.at[n], xr_sem.at[n - 1], at(dx=-dx, dy=-dy))

    ring_sum(1)
    for p in rest:
        pair_tile(*p)
    core_send()
    for s in range(2, half + 1):
        ring_sum(s)
        if s - 2 < tiles:
            plane_send(s - 2)
    for t in range(max(half - 1, 0), tiles):
        plane_send(t)

    emb_i = zbuf[0].astype(f32)
    emb_t = pbuf[0, 0].astype(f32)
    own = temper[0] * jnp.sum(emb_i * emb_t, axis=1, keepdims=True) + bias[0]
    own = (-1.0 / (1.0 + jnp.exp(own))).astype(bf16).astype(f32)
    factor = loss_scale[0] * temper[0] / (LRN * nz * NX * NC)

    def finish(side, total, other):
        grad = jnp.where(live, factor * (total + own * other), 0.0)
        inner = sum(
            jnp.sum(unit[k, side] * grad[:, k * col_w:(k + 1) * col_w], axis=1, keepdims=True)
            for k in range(ny)
        )
        for k in range(ny):
            part = grad[:, k * col_w:(k + 1) * col_w]
            gp[k, side] = (norm[side] * (part - unit[k, side] * inner)).astype(bf16)

    for n in range(1, len(order)):
        arrived(rxy.at[n], xr_sem.at[n - 1])
    total = gtxt[0, 0]
    for n in range(1, len(order)):
        total = total + rxy[n].astype(f32)
    finish(1, total, emb_i)
    total = gimg[0]
    for h in range(ZCH):
        rows = pl.ds(h * zrows, zrows)
        arrived(rz_up.at[half - 1, rows], zr_up.at[half - 1, h])
        if nz - half > 1:
            arrived(rz_dn.at[nz - half - 2, rows], zr_dn.at[nz - half - 2, h])
    total = total + rz_up[half - 1]
    if nz - half > 1:
        total = total + rz_dn[nz - half - 2]
    finish(0, total, emb_t)

    for dy in range(1, ny):
        send(gp.at[(y + dy) % ny], gpr.at[y], yb_sem.at[dy - 1], at(dy=dy))
    gpr[y] = gp[y]
    for dy in range(1, ny):
        arrived(gpr.at[(y - dy + ny) % ny], yb_sem.at[dy - 1])
    for side in range(2):
        grad = gpr[:, side].reshape(ny * slots, col_w)
        gw[side] = dot(feats[side], grad, 0, 0).reshape(gw.shape[1:])

    send(gw.at[:, :, :, 1 - c], gwc, fc_sem, at(dc=1))
    arrived(gwc, fc_sem)
    gx[...] = gw[:, :, :, c] + gwc[...]
    for dx in range(1, NX):
        send(gx.at[:, :, (x + dx) % NX], gxr.at[dx - 1], fx_sem.at[dx - 1], at(dx=dx))
    total = gx[:, :, x]
    for dx in range(1, NX):
        arrived(gxr.at[dx - 1], fx_sem.at[dx - 1])
        total = total + gxr[dx - 1]
    gz[...] = total
    for dz in range(1, nz):
        send(gz.at[:, (z + dz) % nz], gzr.at[dz - 1], fz_sem.at[dz - 1], at(dz=dz))
    total = gz[:, z]
    for dz in range(1, nz):
        arrived(gzr.at[dz - 1], fz_sem.at[dz - 1])
        total = total + gzr[dz - 1]
    out_img[...] = total[0]
    out_txt[...] = total[1]
    for copy in sends:
        copy.wait_send()


def on_device(
    pool_img, pool_txt, w_img, w_txt, logit_scale, logit_bias, loss_scale, select, counts
):
    ny = lax.axis_size("tower")
    rows_n = lax.axis_size("rows")
    nz = rows_n // (NX * NC)
    chips = NX * ny
    list_len = select.shape[0]
    slots = list_len // ny
    depth, col_w = w_img.shape
    emb_w = col_w * ny
    out_rows = depth // rows_n
    half = nz // 2
    vmem, smem = pltpu.VMEM, pltpu.SMEM
    dma = pltpu.SemaphoreType.DMA
    out = jax.ShapeDtypeStruct((out_rows, col_w), f32)
    scratch = [
        vmem((2, list_len, depth), bf16),
        vmem((2, list_len, col_w), f32),
        vmem((ny, 2, slots, col_w), f32),
        vmem((2, slots, 1), f32),
        vmem((nz, slots, emb_w), bf16),
        vmem((chips, NC, slots, emb_w), bf16),
        vmem((nz, slots, emb_w), f32),
        vmem((chips, NC, slots, emb_w), f32),
        vmem((half, slots, emb_w), f32),
        vmem((max(nz - half - 1, 1), slots, emb_w), f32),
        vmem((chips, slots, emb_w), f32),
        vmem((chips, slots, emb_w), f32),
        vmem((chips, slots, emb_w), f32),
        vmem((ny, 2, slots, col_w), bf16),
        vmem((ny, 2, slots, col_w), bf16),
        vmem((2, nz, NX, NC, out_rows, col_w), f32),
        vmem((2, nz, NX, out_rows, col_w), f32),
        vmem((2, nz, NX, out_rows, col_w), f32),
        vmem((NX - 1, 2, nz, out_rows, col_w), f32),
        vmem((2, nz, out_rows, col_w), f32),
        vmem((nz - 1, 2, out_rows, col_w), f32),
        dma((ny - 1, 2)),
        dma((half, ZCH, 2)),
        dma((max(nz - half - 1, 1), ZCH, 2)),
        dma((chips - 1, 2)),
        dma((chips, 2)),
        dma((half, ZCH, 2)),
        dma((max(nz - half - 1, 1), ZCH, 2)),
        dma((chips // TILE, 2)),
        dma((chips - 1, 2)),
        dma((ny - 1, 2)),
        dma((2,)),
        dma((NX - 1, 2)),
        dma((nz - 1, 2)),
    ]
    whole = pl.BlockSpec(memory_space=vmem)
    scalar = pl.BlockSpec(memory_space=smem)
    return pl.pallas_call(
        functools.partial(kernel, (nz, ny, chips)),
        out_shape=(out, out),
        in_specs=[whole] * 5 + [scalar] * 4,
        out_specs=(whole, whole),
        scratch_shapes=scratch,
        compiler_params=pltpu.CompilerParams(
            collective_id=0, has_side_effects=True, vmem_limit_bytes=60 << 20
        ),
        name="learner_step",
    )(
        pool_img, pool_txt, w_img, w_txt, select[:, None], counts,
        logit_scale, logit_bias, loss_scale,
    )


def solution(mesh):
    in_specs = (
        P("rows", None),
        P("rows", None),
        P(None, "tower"),
        P(None, "tower"),
        P(),
        P(),
        P(),
        P("rows"),
        P("rows"),
    )
    out_specs = (P("rows", "tower"), P("rows", "tower"))
    return jax.shard_map(
        on_device, mesh=mesh, in_specs=in_specs, out_specs=out_specs, check_vma=False
    )
```

```python
import functools

import jax
import jax.numpy as jnp
from jax import lax
from jax.experimental import pallas as pl
from jax.experimental.pallas import tpu as pltpu
from jax.sharding import PartitionSpec as P

bf16 = jnp.bfloat16
f32 = jnp.float32
eps = 1e-06

NX, NC = 4, 2
LRN = 128
GROUP, TILE = 4, 4
ZCH = 2
NEAR_Z = 2


def dot(a, b, ca=1, cb=0):
    return lax.dot_general(a, b, (((ca,), (cb,)), ((), ())), preferred_element_type=f32)


def chip_order(nx, ny):
    ring = lambda d, n: min(d, n - d)
    places = [(dx, dy) for dx in range(nx) for dy in range(ny)]
    return sorted(places, key=lambda p: (ring(p[0], nx) + ring(p[1], ny), p))


def kernel(
    cfg,
    h_pool_img, h_pool_txt, h_w_img, h_w_txt, h_sel, h_cnt, h_temper, h_bias, h_loss_scale,
    out_img, out_txt,
    pool, w, sel, cnt, temper, bias, loss_scale,
    feats, feats_t, proj, unit, norm, zbuf, pbuf, gimg, gtxt, rs_out, rs_up, rs_dn,
    rcore, sbuf, rxy, gp, gpr, gw, gwc, gx, gxr, gz, gzr,
    in_sem, y_sem, za_up, za_dn, xy_sem, cf_sem, zr_up, zr_dn, cr_sem, xr_sem, yb_sem,
    fc_sem, fx_sem, fz_sem,
):
    nz, ny = cfg
    row, y = lax.axis_index("rows"), lax.axis_index("tower")
    c = row % NC
    x = row // NC % NX
    z = row // (NC * NX)
    most_up, most_dn = nz // 2, nz - nz // 2 - 1
    order = chip_order(NX, ny)
    groups, tiles = nz // GROUP, len(order) // TILE
    slots = unit.shape[1]
    emb_w = zbuf.shape[2]
    col_w = proj.shape[2]
    sends = []

    def at(dz=0, dx=0, dy=0, dc=0):
        r = ((z + dz + nz) % nz * NX + (x + dx + NX) % NX) * NC + (c + dc) % NC
        return (r, (y + dy + ny) % ny)

    def send(src, dst, sems, where):
        copy = pltpu.make_async_remote_copy(
            src_ref=src, dst_ref=dst, send_sem=sems.at[0], recv_sem=sems.at[1],
            device_id=where, device_id_type=pl.DeviceIdType.MESH,
        )
        copy.start()
        sends.append(copy)

    def arrived(ref, sems):
        pltpu.make_async_remote_copy(
            src_ref=ref, dst_ref=ref, send_sem=sems.at[0], recv_sem=sems.at[1],
            device_id=at(), device_id_type=pl.DeviceIdType.MESH,
        ).wait_recv()

    loads = [
        pltpu.make_async_copy(src, dst, in_sem.at[n])
        for n, (src, dst) in enumerate((
            (h_sel, sel), (h_pool_img, pool.at[0]), (h_w_img, w.at[0]),
            (h_pool_txt, pool.at[1]), (h_w_txt, w.at[1]), (h_cnt, cnt),
            (h_temper, temper), (h_bias, bias), (h_loss_scale, loss_scale),
        ))
    ]
    for load in loads:
        load.start()
    partners = [at(dx=dx, dy=dy) for dx, dy in order[1:]]
    partners += [at(dz=dz) for dz in [d for d in range(1, nz) if min(d, nz - d) <= NEAR_Z]] + [at(dc=1)]
    barrier = pltpu.get_barrier_semaphore()
    for there in partners:
        pl.semaphore_signal(
            barrier, inc=1, device_id=there, device_id_type=pl.DeviceIdType.MESH
        )

    loads[0].wait()
    rows_at = lax.broadcasted_iota(jnp.int32, (pool.shape[1], sel.shape[0]), 0)
    pick = jnp.where(sel[...][None, :] == rows_at, 1.0, 0.0).astype(bf16)

    def project(side):
        loads[1 + 2 * side].wait()
        feats[side] = dot(pick, pool[side], 0, 0).astype(bf16)
        loads[2 + 2 * side].wait()
        proj[side] = dot(feats[side], w[side])

    def deal(side):
        for dy in (2, 1, 3):
            if dy >= ny:
                continue
            yy = (y + dy) % ny
            send(
                proj.at[side, pl.ds(pl.multiple_of(yy * slots, slots), slots)],
                unit.at[side * ny + y], y_sem.at[side, dy - 1], at(dy=dy),
            )
        unit[side * ny + y] = proj[side, pl.ds(pl.multiple_of(y * slots, slots), slots)]

    def embed(side):
        for dy in range(1, ny):
            arrived(unit.at[side * ny + (y - dy + ny) % ny], y_sem.at[side, dy - 1])
        parts = [unit[side * ny + k] for k in range(ny)]
        square = sum(jnp.sum(part * part, axis=1, keepdims=True) for part in parts)
        norm[side] = lax.rsqrt(square + eps)
        for k in range(ny):
            rows = parts[k] * norm[side]
            unit[side * ny + k] = rows
            emb = jnp.where(live, rows, 0.0).astype(bf16)
            if side == 0:
                zbuf[0, :, k * col_w:(k + 1) * col_w] = emb
            else:
                pbuf[0, 0, :, k * col_w:(k + 1) * col_w] = emb

    def spot(offset):
        return 2 * offset if offset >= 0 else -2 * offset - 1

    zrows = slots // ZCH

    def ring_send(p):
        k = 2 * p - 2
        for h in range(ZCH):
            rows = pl.ds(h * zrows, zrows)
            for sign, most, sems in ((1, most_up, za_up), (-1, most_dn, za_dn)):
                if k > most:
                    continue
                have = zbuf.at[spot(-sign * k), rows]
                if k:
                    arrived(have, sems.at[k - 1, h])
                for step in (2, 1):
                    if k + step <= most:
                        send(have, zbuf.at[spot(-sign * (k + step)), rows],
                             sems.at[k + step - 1, h], at(dz=sign * step))

    def ring_odd(p):
        k = 2 * p - 1
        for h in range(ZCH):
            rows = pl.ds(h * zrows, zrows)
            for sign, most, sems in ((1, most_up, za_up), (-1, most_dn, za_dn)):
                if k <= most:
                    arrived(zbuf.at[spot(-sign * k), rows], sems.at[k - 1, h])

    def spread():
        for n, (dx, dy) in enumerate(order[1:]):
            send(pbuf.at[0, 0], pbuf.at[n + 1, 0], xy_sem.at[n], at(dx=dx, dy=dy))
        send(pbuf.at[0, 0], pbuf.at[0, 1], cf_sem.at[0], at(dc=1))

    def hand_over(t):
        for n in range(t * TILE, (t + 1) * TILE):
            if n:
                arrived(pbuf.at[n, 0], xy_sem.at[n - 1])
                send(pbuf.at[n, 0], pbuf.at[n, 1], cf_sem.at[n], at(dc=1))

    def tile_ready(t):
        for n in range(t * TILE, (t + 1) * TILE):
            arrived(pbuf.at[n, 1], cf_sem.at[n])

    def pair_tile(g, t):
        img = zbuf[g * GROUP:(g + 1) * GROUP].reshape(GROUP * slots, emb_w)
        txt = pbuf[t * TILE:(t + 1) * TILE].reshape(TILE * NC * slots, emb_w)
        logits = temper[0] * dot(img, txt, 1, 1) + bias[0]
        weights = 1.0 / (1.0 + jnp.exp(-logits))
        if g == 0 and t == 0:
            i = lax.broadcasted_iota(jnp.int32, logits.shape, 0)
            j = lax.broadcasted_iota(jnp.int32, logits.shape, 1)
            weights = jnp.where((i == j) & (i < slots), 0.0, weights)
        weights = weights.astype(bf16)
        to_img = dot(weights, txt).reshape(GROUP, slots, emb_w)
        to_txt = dot(weights, img, 0, 0).reshape(TILE, NC, slots, emb_w)
        at_img = slice(g * GROUP, (g + 1) * GROUP)
        at_txt = slice(t * TILE, (t + 1) * TILE)
        gimg[at_img] = gimg[at_img] + to_img if g in begun_img else to_img
        gtxt[at_txt] = gtxt[at_txt] + to_txt if t in begun_txt else to_txt
        begun_img.add(g)
        begun_txt.add(t)

    begun_img, begun_txt = set(), set()

    def ring_sum(p):
        k = most_up + 2 - 2 * p
        for h in range(ZCH):
            rows = pl.ds(h * zrows, zrows)
            total = None
            for sign, most, got, sems in (
                (1, most_up, rs_up, zr_up), (-1, most_dn, rs_dn, zr_dn)
            ):
                if k <= most:
                    here = spot(sign * k) if k < most_up else spot(-most_up)
                    if total is None or k:
                        total = gimg[here, rows]
                    for far in (k + 1, k + 2):
                        if far <= most:
                            arrived(got.at[far - 1, rows], sems.at[far - 1, h])
                            total = total + got[far - 1, rows].astype(f32)
                    if k:
                        rs_out[here, rows] = total.astype(bf16)
                        send(rs_out.at[here, rows], got.at[k - 1, rows],
                             sems.at[k - 1, h], at(dz=2 * sign))
                if 1 <= k - 1 <= most:
                    here = spot(sign * (k - 1))
                    rs_out[here, rows] = gimg[here, rows].astype(bf16)
                    send(rs_out.at[here, rows], got.at[k - 2, rows],
                         sems.at[k - 2, h], at(dz=sign))
            if k == 0:
                gimg[0, rows] = total

    def core_send(t):
        part = pl.ds(t * TILE, TILE)
        send(gtxt.at[part, 1], rcore.at[part], cr_sem.at[t], at(dc=1))

    def plane_send(t):
        part = pl.ds(t * TILE, TILE)
        arrived(rcore.at[part], cr_sem.at[t])
        for n in range(t * TILE, (t + 1) * TILE):
            both = gtxt[n, 0] + rcore[n]
            if n == 0:
                gtxt[0, 0] = both
            else:
                sbuf[n] = both.astype(sbuf.dtype)
                dx, dy = order[n]
                send(sbuf.at[n], rxy.at[n], xr_sem.at[n - 1], at(dx=-dx, dy=-dy))

    def finish(side, total, emb, other):
        own = temper[0] * jnp.sum(emb * other, axis=1, keepdims=True) + bias[0]
        own = (-1.0 / (1.0 + jnp.exp(own))).astype(bf16).astype(f32)
        factor = loss_scale[0] * temper[0] / (LRN * nz * NX * NC)
        grad = jnp.where(live, factor * (total + own * other), 0.0)
        inner = sum(
            jnp.sum(unit[side * ny + k] * grad[:, k * col_w:(k + 1) * col_w],
                    axis=1, keepdims=True)
            for k in range(ny)
        )
        for k in range(ny):
            part = grad[:, k * col_w:(k + 1) * col_w]
            gp[side * ny + k] = (
                norm[side] * (part - unit[side * ny + k] * inner)
            ).astype(bf16)
        for dy in (2, 1, 3):
            if dy < ny:
                send(gp.at[side * ny + (y + dy) % ny], gpr.at[side * ny + y],
                     yb_sem.at[side, dy - 1], at(dy=dy))
        gpr[side * ny + y] = gp[side * ny + y]

    def weight_grad(side):
        for dy in range(1, ny):
            arrived(gpr.at[side * ny + (y - dy + ny) % ny], yb_sem.at[side, dy - 1])
        grad = gpr[side * ny:(side + 1) * ny].reshape(ny * slots, col_w)
        gw[side] = dot(feats_t[side], grad).reshape(gw.shape[1:])
        send(gw.at[side, :, :, 1 - c], gwc.at[side], fc_sem.at[side], at(dc=1))

    def over_x(side):
        arrived(gwc.at[side], fc_sem.at[side])
        gx[side] = gw[side, :, :, c] + gwc[side]
        for dx in (2, 1, 3):
            if dx < NX:
                send(gx.at[side, :, (x + dx) % NX], gxr.at[side, dx - 1],
                     fx_sem.at[side, dx - 1], at(dx=dx))

    def over_z(side):
        total = gx[side, :, x]
        for dx in range(1, NX):
            arrived(gxr.at[side, dx - 1], fx_sem.at[side, dx - 1])
            total = total + gxr[side, dx - 1]
        gz[side] = total
        for dz in sorted(range(1, nz), key=lambda d: -min(d, nz - d)):
            send(gz.at[side, (z + dz) % nz], gzr.at[side, dz - 1],
                 fz_sem.at[side, dz - 1], at(dz=dz))

    def collect(side, out):
        total = gz[side, z]
        for dz in range(1, nz):
            arrived(gzr.at[side, dz - 1], fz_sem.at[side, dz - 1])
            total = total + gzr[side, dz - 1]
        out[...] = total

    project(0)
    for load in loads[5:]:
        load.wait()
    slot_at = y * slots + lax.broadcasted_iota(jnp.int32, (slots, 1), 0)
    live = slot_at < cnt[0]
    pl.semaphore_wait(barrier, len(partners))
    deal(0)
    project(1)
    deal(1)
    embed(0)
    ring_send(1)
    embed(1)
    spread()
    for side in range(2):
        feats_t[side] = feats[side].T

    phases = [
        [(k, t) for t in range(k)] + [(g, k) for g in range(k + 1)] for k in range(groups - 1)
    ]
    phases.append([(groups - 1, t) for t in range(tiles)])
    opened = 0
    for p in range(1, most_up // 2 + 2):
        if p > 1:
            ring_send(p)
            ring_odd(p - 1)
        queue = []
        while opened < groups and p > 1 and (
            (opened + 1) * GROUP - 1 <= min(4 * (p - 1), nz - 1)
        ):
            if opened >= p - 1 and opened:
                hand_over(opened)
            tile_ready(opened)
            queue += phases[opened]
            opened += 1
        if p <= most_up // 2:
            for tile in queue:
                pair_tile(*tile)
            if p <= tiles:
                hand_over(p - 1)
    early = [tile for tile in queue if tile[0] < groups - 1]
    for tile in early:
        pair_tile(*tile)
    for t in range(tiles):
        pair_tile(groups - 1, t)
        if t < tiles - 1:
            core_send(t)
    ring_sum(1)
    for g in range(groups - 2, -1, -1):
        pair_tile(g, tiles - 1)
    core_send(tiles - 1)
    done = 0
    for p in range(2, most_up // 2 + 1):
        for t in range(done, min(done + 2, tiles)):
            plane_send(t)
        done = min(done + 2, tiles)
        ring_sum(p)
    for t in range(done, tiles):
        plane_send(t)
    emb_i = zbuf[0].astype(f32)
    emb_t = pbuf[0, 0].astype(f32)
    for n in range(1, len(order)):
        arrived(rxy.at[n], xr_sem.at[n - 1])
    total = gtxt[0, 0]
    for n in range(1, len(order)):
        total = total + rxy[n].astype(f32)
    finish(1, total, emb_t, emb_i)
    ring_sum(most_up // 2 + 1)
    finish(0, gimg[0], emb_i, emb_t)
    weight_grad(1)
    weight_grad(0)
    over_x(1)
    over_x(0)
    over_z(1)
    over_z(0)
    collect(1, out_txt)
    collect(0, out_img)
    for copy in sends:
        copy.wait_send()


def on_device(
    pool_img, pool_txt, w_img, w_txt, logit_scale, logit_bias, loss_scale, select, counts
):
    ny = lax.axis_size("tower")
    rows_n = lax.axis_size("rows")
    nz = rows_n // (NX * NC)
    chips = NX * ny
    list_len = select.shape[0]
    slots = list_len // ny
    depth, col_w = w_img.shape
    emb_w = col_w * ny
    out_rows = depth // rows_n
    most_up, most_dn = nz // 2, nz - nz // 2 - 1
    vmem, smem = pltpu.VMEM, pltpu.SMEM
    dma = pltpu.SemaphoreType.DMA
    out = jax.ShapeDtypeStruct((out_rows, col_w), f32)
    scratch = [
        vmem((2,) + pool_img.shape, bf16),
        vmem((2, depth, col_w), bf16),
        vmem((list_len,), jnp.int32),
        smem((1,), jnp.int32),
        smem((1,), f32),
        smem((1,), f32),
        smem((1,), f32),
        vmem((2, list_len, depth), bf16),
        vmem((2, depth, list_len), bf16),
        vmem((2, list_len, col_w), f32),
        vmem((2 * ny, slots, col_w), f32),
        vmem((2, slots, 1), f32),
        vmem((nz, slots, emb_w), bf16),
        vmem((chips, NC, slots, emb_w), bf16),
        vmem((nz, slots, emb_w), f32),
        vmem((chips, NC, slots, emb_w), f32),
        vmem((nz, slots, emb_w), bf16),
        vmem((most_up, slots, emb_w), bf16),
        vmem((most_dn, slots, emb_w), bf16),
        vmem((chips, slots, emb_w), f32),
        vmem((chips, slots, emb_w), bf16),
        vmem((chips, slots, emb_w), bf16),
        vmem((2 * ny, slots, col_w), bf16),
        vmem((2 * ny, slots, col_w), bf16),
        vmem((2, nz, NX, NC, out_rows, col_w), f32),
        vmem((2, nz, NX, out_rows, col_w), f32),
        vmem((2, nz, NX, out_rows, col_w), f32),
        vmem((2, NX - 1, nz, out_rows, col_w), f32),
        vmem((2, nz, out_rows, col_w), f32),
        vmem((2, nz - 1, out_rows, col_w), f32),
        dma((9,)),
        dma((2, ny - 1, 2)),
        dma((most_up, ZCH, 2)),
        dma((most_dn, ZCH, 2)),
        dma((chips - 1, 2)),
        dma((chips, 2)),
        dma((most_up, ZCH, 2)),
        dma((most_dn, ZCH, 2)),
        dma((chips // TILE, 2)),
        dma((chips - 1, 2)),
        dma((2, ny - 1, 2)),
        dma((2, 2)),
        dma((2, NX - 1, 2)),
        dma((2, nz - 1, 2)),
    ]
    whole = pl.BlockSpec(memory_space=vmem)
    placed = pl.BlockSpec(memory_space=pl.ANY)
    return pl.pallas_call(
        functools.partial(kernel, (nz, ny)),
        out_shape=(out, out),
        in_specs=[placed] * 4 + [pl.BlockSpec(memory_space=pltpu.HBM)] * 5,
        out_specs=(whole, whole),
        scratch_shapes=scratch,
        compiler_params=pltpu.CompilerParams(
            collective_id=0, has_side_effects=True, vmem_limit_bytes=60 << 20
        ),
        name="learner_step",
    )(
        pool_img, pool_txt, w_img, w_txt, select, counts,
        logit_scale, logit_bias, loss_scale,
    )


def solution(mesh):
    in_specs = (
        P("rows", None),
        P("rows", None),
        P(None, "tower"),
        P(None, "tower"),
        P(),
        P(),
        P(),
        P("rows"),
        P("rows"),
    )
    out_specs = (P("rows", "tower"), P("rows", "tower"))
    return jax.shard_map(
        on_device, mesh=mesh, in_specs=in_specs, out_specs=out_specs, check_vma=False
    )
```

```python
import functools

import jax
import jax.numpy as jnp
from jax import lax
from jax.experimental import pallas as pl
from jax.experimental.pallas import tpu as pltpu
from jax.sharding import PartitionSpec as P

bf16 = jnp.bfloat16
f32 = jnp.float32
eps = 1e-06

NX, NC = 4, 2
LRN = 128
PLAN = {
    2: [("hand", 0)],
    3: [("hand", 1), ("ready", 0), ("pair", 0, 0), ("pair", 1, 0),
        ("ready", 1), ("pair", 0, 1), ("pair", 1, 1), ("hand", 2)],
    4: [("hand", 3), ("pair", 2, 0), ("pair", 2, 1),
        ("ready", 2), ("pair", 0, 2), ("pair", 1, 2), ("pair", 2, 2)],
    5: [("ready", 3)],
}
GROUPS, TILE = (0, 5, 9, 13, 16), 4
ZCH = 2
NEAR_Z = 2


def dot(a, b, ca=1, cb=0):
    return lax.dot_general(a, b, (((ca,), (cb,)), ((), ())), preferred_element_type=f32)


def chip_order(nx, ny):
    ring = lambda d, n: min(d, n - d)
    places = [(dx, dy) for dx in range(nx) for dy in range(ny)]
    return sorted(places, key=lambda p: (ring(p[0], nx) + ring(p[1], ny), p))


def kernel(
    cfg,
    h_pool_img, h_pool_txt, h_w_img, h_w_txt, h_sel, cnt, temper, bias, loss_scale,
    out_img, out_txt,
    pool, w, sel,
    feats, feats_t, proj, unit, norm, zbuf, pbuf, gimg, gtxt, rs_out, rs_up, rs_dn,
    rcore, sbuf, rxy, gp, gpr, gw, gwc, gx, gxr, gz, gzr,
    in_sem, y_sem, za_up, za_dn, xy_sem, cf_sem, zr_up, zr_dn, cr_sem, xr_sem, yb_sem,
    fc_sem, fx_sem, fz_sem,
):
    nz, ny = cfg
    row, y = lax.axis_index("rows"), lax.axis_index("tower")
    c = row % NC
    x = row // NC % NX
    z = row // (NC * NX)
    most_up = nz // 2
    order = chip_order(NX, ny)
    groups, tiles = len(GROUPS) - 1, len(order) // TILE
    slots = unit.shape[1]
    emb_w = zbuf.shape[2]
    col_w = proj.shape[2]
    sends = []

    def at(dz=0, dx=0, dy=0, dc=0):
        r = ((z + dz + nz) % nz * NX + (x + dx + NX) % NX) * NC + (c + dc) % NC
        return (r, (y + dy + ny) % ny)

    def send(src, dst, sems, where):
        copy = pltpu.make_async_remote_copy(
            src_ref=src, dst_ref=dst, send_sem=sems.at[0], recv_sem=sems.at[1],
            device_id=where, device_id_type=pl.DeviceIdType.MESH,
        )
        copy.start()
        sends.append(copy)

    def arrived(ref, sems):
        pltpu.make_async_remote_copy(
            src_ref=ref, dst_ref=ref, send_sem=sems.at[0], recv_sem=sems.at[1],
            device_id=at(), device_id_type=pl.DeviceIdType.MESH,
        ).wait_recv()

    loads = [
        pltpu.make_async_copy(src, dst, in_sem.at[n])
        for n, (src, dst) in enumerate((
            (h_sel, sel), (h_pool_img, pool.at[0]), (h_w_img, w.at[0]),
            (h_pool_txt, pool.at[1]), (h_w_txt, w.at[1]),
        ))
    ]
    for load in loads:
        load.start()
    partners = [at(dx=dx, dy=dy) for dx, dy in order[1:]]
    partners += [at(dz=dz) for dz in [d for d in range(1, nz) if min(d, nz - d) <= NEAR_Z]] + [at(dc=1)]
    barrier = pltpu.get_barrier_semaphore()
    for there in partners:
        pl.semaphore_signal(
            barrier, inc=1, device_id=there, device_id_type=pl.DeviceIdType.MESH
        )

    loads[0].wait()
    rows_at = lax.broadcasted_iota(jnp.int32, (pool.shape[1], sel.shape[0]), 0)
    pick = jnp.where(sel[...][None, :] == rows_at, 1.0, 0.0).astype(bf16)

    def project(side):
        loads[1 + 2 * side].wait()
        feats[side] = dot(pick, pool[side], 0, 0).astype(bf16)
        loads[2 + 2 * side].wait()
        proj[side] = dot(feats[side], w[side])

    def deal(side):
        for dy in (2, 1, 3):
            if dy >= ny:
                continue
            yy = (y + dy) % ny
            send(
                proj.at[side, pl.ds(pl.multiple_of(yy * slots, slots), slots)],
                unit.at[side * ny + y], y_sem.at[side, dy - 1], at(dy=dy),
            )
        unit[side * ny + y] = proj[side, pl.ds(pl.multiple_of(y * slots, slots), slots)]

    def embed(side):
        for dy in range(1, ny):
            arrived(unit.at[side * ny + (y - dy + ny) % ny], y_sem.at[side, dy - 1])
        parts = [unit[side * ny + k] for k in range(ny)]
        square = sum(jnp.sum(part * part, axis=1, keepdims=True) for part in parts)
        norm[side] = lax.rsqrt(square + eps)
        for k in range(ny):
            rows = parts[k] * norm[side]
            unit[side * ny + k] = rows
            emb = jnp.where(live, rows, 0.0).astype(bf16)
            if side == 0:
                zbuf[0, :, k * col_w:(k + 1) * col_w] = emb
            else:
                pbuf[0, 0, :, k * col_w:(k + 1) * col_w] = emb

    def spot(offset):
        return 2 * offset if 0 <= offset < most_up else 2 * abs(offset) - 1

    zrows = slots // ZCH

    def ways(h, *args):
        up = h < ZCH // 2
        return [
            (1, most_up - (not up), *args[0::2]), (-1, most_up - up, *args[1::2])
        ]

    def ring_send(p):
        k = 2 * p - 2
        for h in range(ZCH):
            rows = pl.ds(h * zrows, zrows)
            for sign, most, sems in ways(h, za_up, za_dn):
                if k > most:
                    continue
                have = zbuf.at[spot(-sign * k), rows]
                if k:
                    arrived(have, sems.at[k - 1, h])
                for step in (2, 1):
                    if k + step <= most:
                        send(have, zbuf.at[spot(-sign * (k + step)), rows],
                             sems.at[k + step - 1, h], at(dz=sign * step))

    def ring_odd(p):
        k = 2 * p - 1
        for h in range(ZCH):
            rows = pl.ds(h * zrows, zrows)
            for sign, most, sems in ways(h, za_up, za_dn):
                if k <= most:
                    arrived(zbuf.at[spot(-sign * k), rows], sems.at[k - 1, h])

    def spread():
        for n, (dx, dy) in enumerate(order[1:]):
            send(pbuf.at[0, 0], pbuf.at[n + 1, 0], xy_sem.at[n], at(dx=dx, dy=dy))
        send(pbuf.at[0, 0], pbuf.at[0, 1], cf_sem.at[0], at(dc=1))

    def hand_over(t):
        for n in range(t * TILE, (t + 1) * TILE):
            if n:
                arrived(pbuf.at[n, 0], xy_sem.at[n - 1])
                send(pbuf.at[n, 0], pbuf.at[n, 1], cf_sem.at[n], at(dc=1))

    def tile_ready(t):
        for n in range(t * TILE, (t + 1) * TILE):
            arrived(pbuf.at[n, 1], cf_sem.at[n])

    def pair_tile(g, t):
        at_img = slice(GROUPS[g], GROUPS[g + 1])
        count = GROUPS[g + 1] - GROUPS[g]
        img = zbuf[at_img].reshape(count * slots, emb_w)
        txt = pbuf[t * TILE:(t + 1) * TILE].reshape(TILE * NC * slots, emb_w)
        logits = temper_val * dot(img, txt, 1, 1) + bias_val
        weights = 1.0 / (1.0 + jnp.exp(-logits))
        if g == 0 and t == 0:
            i = lax.broadcasted_iota(jnp.int32, logits.shape, 0)
            j = lax.broadcasted_iota(jnp.int32, logits.shape, 1)
            weights = jnp.where((i == j) & (i < slots), 0.0, weights)
        weights = weights.astype(bf16)
        to_img = dot(weights, txt).reshape(count, slots, emb_w)
        to_txt = dot(weights, img, 0, 0).reshape(TILE, NC, slots, emb_w)
        at_txt = slice(t * TILE, (t + 1) * TILE)
        gimg[at_img] = gimg[at_img] + to_img if g in begun_img else to_img
        gtxt[at_txt] = gtxt[at_txt] + to_txt if t in begun_txt else to_txt
        begun_img.add(g)
        begun_txt.add(t)

    begun_img, begun_txt = set(), set()

    def ring_sum(p):
        k = most_up + 2 - 2 * p
        for h in range(ZCH):
            rows = pl.ds(h * zrows, zrows)
            total = None
            for sign, most, got, sems in ways(h, rs_up, rs_dn, zr_up, zr_dn):
                if k <= most:
                    here = spot(sign * k)
                    if total is None or k:
                        total = gimg[here, rows]
                    for far in (k + 1, k + 2):
                        if far <= most:
                            arrived(got.at[far - 1, rows], sems.at[far - 1, h])
                            total = total + got[far - 1, rows].astype(f32)
                    if k:
                        rs_out[here, rows] = total.astype(bf16)
                        send(rs_out.at[here, rows], got.at[k - 1, rows],
                             sems.at[k - 1, h], at(dz=2 * sign))
                if 1 <= k - 1 <= most:
                    here = spot(sign * (k - 1))
                    rs_out[here, rows] = gimg[here, rows].astype(bf16)
                    send(rs_out.at[here, rows], got.at[k - 2, rows],
                         sems.at[k - 2, h], at(dz=sign))
            if k == 0:
                gimg[0, rows] = total

    def core_send(t):
        part = pl.ds(t * TILE, TILE)
        send(gtxt.at[part, 1], rcore.at[part], cr_sem.at[t], at(dc=1))

    def plane_send(t):
        part = pl.ds(t * TILE, TILE)
        arrived(rcore.at[part], cr_sem.at[t])
        for n in range(t * TILE, (t + 1) * TILE):
            both = gtxt[n, 0] + rcore[n]
            if n == 0:
                gtxt[0, 0] = both
            else:
                sbuf[n] = both.astype(sbuf.dtype)
                dx, dy = order[n]
                send(sbuf.at[n], rxy.at[n], xr_sem.at[n - 1], at(dx=-dx, dy=-dy))

    def finish(side, total, emb, other):
        own = temper_val * jnp.sum(emb * other, axis=1, keepdims=True) + bias_val
        own = (-1.0 / (1.0 + jnp.exp(own))).astype(bf16).astype(f32)
        grad = jnp.where(live, factor * (total + own * other), 0.0)
        inner = sum(
            jnp.sum(unit[side * ny + k] * grad[:, k * col_w:(k + 1) * col_w],
                    axis=1, keepdims=True)
            for k in range(ny)
        )
        for k in range(ny):
            part = grad[:, k * col_w:(k + 1) * col_w]
            gp[side * ny + k] = (
                norm[side] * (part - unit[side * ny + k] * inner)
            ).astype(bf16)
        for dy in (2, 1, 3):
            if dy < ny:
                send(gp.at[side * ny + (y + dy) % ny], gpr.at[side * ny + y],
                     yb_sem.at[side, dy - 1], at(dy=dy))
        gpr[side * ny + y] = gp[side * ny + y]

    def weight_grad(side):
        for dy in range(1, ny):
            arrived(gpr.at[side * ny + (y - dy + ny) % ny], yb_sem.at[side, dy - 1])
        grad = gpr[side * ny:(side + 1) * ny].reshape(ny * slots, col_w)
        gw[side] = dot(feats_t[side], grad).reshape(gw.shape[1:])
        send(gw.at[side, :, :, 1 - c], gwc.at[side], fc_sem.at[side], at(dc=1))

    def over_x(side):
        arrived(gwc.at[side], fc_sem.at[side])
        gx[side] = gw[side, :, :, c] + gwc[side]
        for dx in (2, 1, 3):
            if dx < NX:
                send(gx.at[side, :, (x + dx) % NX], gxr.at[side, dx - 1],
                     fx_sem.at[side, dx - 1], at(dx=dx))

    def over_z(side):
        total = gx[side, :, x]
        for dx in range(1, NX):
            arrived(gxr.at[side, dx - 1], fx_sem.at[side, dx - 1])
            total = total + gxr[side, dx - 1]
        gz[side] = total
        for dz in sorted(range(1, nz), key=lambda d: -min(d, nz - d)):
            send(gz.at[side, (z + dz) % nz], gzr.at[side, dz - 1],
                 fz_sem.at[side, dz - 1], at(dz=dz))

    def collect(side, out):
        total = gz[side, z]
        for dz in range(1, nz):
            arrived(gzr.at[side, dz - 1], fz_sem.at[side, dz - 1])
            total = total + gzr[side, dz - 1]
        out[...] = total

    project(0)
    temper_val, bias_val = temper[0], bias[0]
    factor = loss_scale[0] * temper_val / (LRN * nz * NX * NC)
    slot_at = y * slots + lax.broadcasted_iota(jnp.int32, (slots, 1), 0)
    live = slot_at < cnt[0]
    pl.semaphore_wait(barrier, len(partners))
    deal(0)
    project(1)
    deal(1)
    embed(0)
    ring_send(1)
    embed(1)
    spread()
    for side in range(2):
        feats_t[side] = feats[side].T

    for p in range(2, most_up // 2 + 2):
        ring_send(p)
        ring_odd(p - 1)
        for what, *which in PLAN[p]:
            {"hand": hand_over, "ready": tile_ready, "pair": pair_tile}[what](*which)
    for t in range(tiles):
        pair_tile(groups - 1, t)
        if t < tiles - 1:
            core_send(t)
    ring_sum(1)
    for g in range(groups - 2, -1, -1):
        pair_tile(g, tiles - 1)
    core_send(tiles - 1)
    done = 0
    for p in range(2, most_up // 2 + 1):
        for t in range(done, min(done + 2, tiles)):
            plane_send(t)
        done = min(done + 2, tiles)
        ring_sum(p)
    for t in range(done, tiles):
        plane_send(t)
    emb_i = zbuf[0].astype(f32)
    emb_t = pbuf[0, 0].astype(f32)
    for n in range(1, len(order)):
        arrived(rxy.at[n], xr_sem.at[n - 1])
    total = gtxt[0, 0]
    for n in range(1, len(order)):
        total = total + rxy[n].astype(f32)
    finish(1, total, emb_t, emb_i)
    weight_grad(1)
    ring_sum(most_up // 2 + 1)
    finish(0, gimg[0], emb_i, emb_t)
    over_x(1)
    weight_grad(0)
    over_x(0)
    over_z(1)
    over_z(0)
    collect(1, out_txt)
    collect(0, out_img)
    for copy in sends:
        copy.wait_send()


def on_device(
    pool_img, pool_txt, w_img, w_txt, logit_scale, logit_bias, loss_scale, select, counts
):
    ny = lax.axis_size("tower")
    rows_n = lax.axis_size("rows")
    nz = rows_n // (NX * NC)
    chips = NX * ny
    list_len = select.shape[0]
    slots = list_len // ny
    depth, col_w = w_img.shape
    emb_w = col_w * ny
    out_rows = depth // rows_n
    most_up = nz // 2
    vmem = pltpu.VMEM
    dma = pltpu.SemaphoreType.DMA
    out = jax.ShapeDtypeStruct((out_rows, col_w), f32)
    scratch = [
        vmem((2,) + pool_img.shape, bf16),
        vmem((2, depth, col_w), bf16),
        vmem((list_len,), jnp.int32),
        vmem((2, list_len, depth), bf16),
        vmem((2, depth, list_len), bf16),
        vmem((2, list_len, col_w), f32),
        vmem((2 * ny, slots, col_w), f32),
        vmem((2, slots, 1), f32),
        vmem((nz, slots, emb_w), bf16),
        vmem((chips, NC, slots, emb_w), bf16),
        vmem((nz, slots, emb_w), f32),
        vmem((chips, NC, slots, emb_w), f32),
        vmem((nz, slots, emb_w), bf16),
        vmem((most_up, slots, emb_w), bf16),
        vmem((most_up, slots, emb_w), bf16),
        vmem((chips, slots, emb_w), f32),
        vmem((chips, slots, emb_w), bf16),
        vmem((chips, slots, emb_w), bf16),
        vmem((2 * ny, slots, col_w), bf16),
        vmem((2 * ny, slots, col_w), bf16),
        vmem((2, nz, NX, NC, out_rows, col_w), f32),
        vmem((2, nz, NX, out_rows, col_w), f32),
        vmem((2, nz, NX, out_rows, col_w), f32),
        vmem((2, NX - 1, nz, out_rows, col_w), f32),
        vmem((2, nz, out_rows, col_w), f32),
        vmem((2, nz - 1, out_rows, col_w), f32),
        dma((5,)),
        dma((2, ny - 1, 2)),
        dma((most_up, ZCH, 2)),
        dma((most_up, ZCH, 2)),
        dma((chips - 1, 2)),
        dma((chips, 2)),
        dma((most_up, ZCH, 2)),
        dma((most_up, ZCH, 2)),
        dma((chips // TILE, 2)),
        dma((chips - 1, 2)),
        dma((2, ny - 1, 2)),
        dma((2, 2)),
        dma((2, NX - 1, 2)),
        dma((2, nz - 1, 2)),
    ]
    whole = pl.BlockSpec(memory_space=vmem)
    placed = pl.BlockSpec(memory_space=pl.ANY)
    return pl.pallas_call(
        functools.partial(kernel, (nz, ny)),
        out_shape=(out, out),
        in_specs=[placed] * 5 + [pl.BlockSpec(memory_space=pltpu.SMEM)] * 4,
        out_specs=(whole, whole),
        scratch_shapes=scratch,
        compiler_params=pltpu.CompilerParams(
            collective_id=0, has_side_effects=True, vmem_limit_bytes=60 << 20
        ),
        name="learner_step",
    )(
        pool_img, pool_txt, w_img, w_txt, select, counts,
        logit_scale, logit_bias, loss_scale,
    )


def solution(mesh):
    in_specs = (
        P("rows", None),
        P("rows", None),
        P(None, "tower"),
        P(None, "tower"),
        P(),
        P(),
        P(),
        P("rows"),
        P("rows"),
    )
    out_specs = (P("rows", "tower"), P("rows", "tower"))
    return jax.shard_map(
        on_device, mesh=mesh, in_specs=in_specs, out_specs=out_specs, check_vma=False
    )
```

```python
import functools

import jax
import jax.numpy as jnp
from jax import lax
from jax.experimental import pallas as pl
from jax.experimental.pallas import tpu as pltpu
from jax.sharding import PartitionSpec as P

bf16 = jnp.bfloat16
f32 = jnp.float32
eps = 1e-06

NX, NC = 4, 2
LRN = 128
PLAN = {
    2: [("hand", 0)],
    3: [("hand", 1), ("ready", 0), ("pair", 0, 0), ("pair", 1, 0),
        ("ready", 1), ("pair", 0, 1), ("pair", 1, 1), ("hand", 2)],
    4: [("hand", 3), ("pair", 2, 0), ("pair", 2, 1),
        ("ready", 2), ("pair", 0, 2), ("pair", 1, 2), ("pair", 2, 2)],
    5: [("ready", 3)],
}
GROUPS, TILE = (0, 5, 9, 13, 16), 4
ZCH = 2
PARTS = 4
NEAR_Z = 2


def dot(a, b, ca=1, cb=0):
    return lax.dot_general(a, b, (((ca,), (cb,)), ((), ())), preferred_element_type=f32)


def chip_order(nx, ny):
    ring = lambda d, n: min(d, n - d)
    places = [(dx, dy) for dx in range(nx) for dy in range(ny)]
    return sorted(places, key=lambda p: (ring(p[0], nx) + ring(p[1], ny), p))


def kernel(
    cfg,
    h_pool_img, h_pool_txt, h_w_img, h_w_txt, h_sel, cnt, temper, bias, loss_scale,
    out_img, out_txt,
    pool, w, sel,
    feats, feats_t, proj, unit, norm, zbuf, pbuf, gimg, gtxt, wbuf, rs_out, rs_up, rs_dn,
    rcore, sbuf, rxy, gp, gpr, gw, gwc, gx, gxr, gz, gzr,
    in_sem, y_sem, za_up, za_dn, xy_sem, cf_sem, zr_up, zr_dn, cr_sem, xr_sem, yb_sem,
    fc_sem, fx_sem, fz_sem,
):
    nz, ny = cfg
    row, y = lax.axis_index("rows"), lax.axis_index("tower")
    c = row % NC
    x = row // NC % NX
    z = row // (NC * NX)
    most_up = nz // 2
    order = chip_order(NX, ny)
    groups, tiles = len(GROUPS) - 1, len(order) // TILE
    slots = unit.shape[1]
    emb_w = zbuf.shape[2]
    col_w = proj.shape[2]
    sends = []

    def at(dz=0, dx=0, dy=0, dc=0):
        r = ((z + dz + nz) % nz * NX + (x + dx + NX) % NX) * NC + (c + dc) % NC
        return (r, (y + dy + ny) % ny)

    def send(src, dst, sems, where):
        copy = pltpu.make_async_remote_copy(
            src_ref=src, dst_ref=dst, send_sem=sems.at[0], recv_sem=sems.at[1],
            device_id=where, device_id_type=pl.DeviceIdType.MESH,
        )
        copy.start()
        sends.append(copy)

    def arrived(ref, sems):
        pltpu.make_async_remote_copy(
            src_ref=ref, dst_ref=ref, send_sem=sems.at[0], recv_sem=sems.at[1],
            device_id=at(), device_id_type=pl.DeviceIdType.MESH,
        ).wait_recv()

    loads = [
        pltpu.make_async_copy(src, dst, in_sem.at[n])
        for n, (src, dst) in enumerate((
            (h_sel, sel), (h_pool_img, pool.at[0]), (h_w_img, w.at[0]),
            (h_pool_txt, pool.at[1]), (h_w_txt, w.at[1]),
        ))
    ]
    for load in loads:
        load.start()
    partners = [at(dx=dx, dy=dy) for dx, dy in order[1:]]
    partners += [at(dz=dz) for dz in [d for d in range(1, nz) if min(d, nz - d) <= NEAR_Z]] + [at(dc=1)]
    barrier = pltpu.get_barrier_semaphore()
    for there in partners:
        pl.semaphore_signal(
            barrier, inc=1, device_id=there, device_id_type=pl.DeviceIdType.MESH
        )

    loads[0].wait()
    rows_at = lax.broadcasted_iota(jnp.int32, (pool.shape[1], sel.shape[0]), 0)
    pick = jnp.where(sel[...][None, :] == rows_at, 1.0, 0.0).astype(bf16)

    def project(side):
        loads[1 + 2 * side].wait()
        feats[side] = dot(pick, pool[side], 0, 0).astype(bf16)
        loads[2 + 2 * side].wait()
        proj[side] = dot(feats[side], w[side])

    def deal(side):
        for dy in (2, 1, 3):
            if dy >= ny:
                continue
            yy = (y + dy) % ny
            send(
                proj.at[side, pl.ds(pl.multiple_of(yy * slots, slots), slots)],
                unit.at[side * ny + y], y_sem.at[side, dy - 1], at(dy=dy),
            )
        unit[side * ny + y] = proj[side, pl.ds(pl.multiple_of(y * slots, slots), slots)]

    def embed(side):
        for dy in range(1, ny):
            arrived(unit.at[side * ny + (y - dy + ny) % ny], y_sem.at[side, dy - 1])
        parts = [unit[side * ny + k] for k in range(ny)]
        square = sum(jnp.sum(part * part, axis=1, keepdims=True) for part in parts)
        norm[side] = lax.rsqrt(square + eps)
        for k in range(ny):
            rows = parts[k] * norm[side]
            unit[side * ny + k] = rows
            emb = jnp.where(live, rows, 0.0).astype(bf16)
            if side == 0:
                zbuf[0, :, k * col_w:(k + 1) * col_w] = emb
            else:
                pbuf[0, 0, :, k * col_w:(k + 1) * col_w] = emb

    def spot(offset):
        return 2 * offset if 0 <= offset < most_up else 2 * abs(offset) - 1

    zrows = slots // ZCH

    def ways(h, *args):
        up = h < ZCH // 2
        return [
            (1, most_up - (not up), *args[0::2]), (-1, most_up - up, *args[1::2])
        ]

    def ring_send(p):
        k = 2 * p - 2
        for h in range(ZCH):
            rows = pl.ds(h * zrows, zrows)
            for sign, most, sems in ways(h, za_up, za_dn):
                if k > most:
                    continue
                have = zbuf.at[spot(-sign * k), rows]
                if k:
                    arrived(have, sems.at[k - 1, h])
                for step in (2, 1):
                    if k + step <= most:
                        send(have, zbuf.at[spot(-sign * (k + step)), rows],
                             sems.at[k + step - 1, h], at(dz=sign * step))

    def ring_odd(p):
        k = 2 * p - 1
        for h in range(ZCH):
            rows = pl.ds(h * zrows, zrows)
            for sign, most, sems in ways(h, za_up, za_dn):
                if k <= most:
                    arrived(zbuf.at[spot(-sign * k), rows], sems.at[k - 1, h])

    def spread():
        for n, (dx, dy) in enumerate(order[1:]):
            send(pbuf.at[0, 0], pbuf.at[n + 1, 0], xy_sem.at[n], at(dx=dx, dy=dy))
        send(pbuf.at[0, 0], pbuf.at[0, 1], cf_sem.at[0], at(dc=1))

    def hand_over(t):
        for n in range(t * TILE, (t + 1) * TILE):
            if n:
                arrived(pbuf.at[n, 0], xy_sem.at[n - 1])
                send(pbuf.at[n, 0], pbuf.at[n, 1], cf_sem.at[n], at(dc=1))

    def tile_ready(t):
        for n in range(t * TILE, (t + 1) * TILE):
            arrived(pbuf.at[n, 1], cf_sem.at[n])

    def pair_tile(g, t, part=None):
        at_img = slice(GROUPS[g], GROUPS[g + 1])
        count = GROUPS[g + 1] - GROUPS[g]
        img = zbuf[at_img].reshape(count * slots, emb_w)
        txt = pbuf[t * TILE:(t + 1) * TILE].reshape(TILE * NC * slots, emb_w)
        at_txt = slice(t * TILE, (t + 1) * TILE)
        if part == "txt":
            to_txt = dot(wbuf[t], img, 0, 0).reshape(TILE, NC, slots, emb_w)
            gtxt[at_txt] = gtxt[at_txt] + to_txt
            return
        logits = temper_val * dot(img, txt, 1, 1) + bias_val
        weights = 1.0 / (1.0 + jnp.exp(-logits))
        if g == 0 and t == 0:
            i = lax.broadcasted_iota(jnp.int32, logits.shape, 0)
            j = lax.broadcasted_iota(jnp.int32, logits.shape, 1)
            weights = jnp.where((i == j) & (i < slots), 0.0, weights)
        weights = weights.astype(bf16)
        to_img = dot(weights, txt).reshape(count, slots, emb_w)
        gimg[at_img] = gimg[at_img] + to_img if g in begun_img else to_img
        begun_img.add(g)
        if part == "img":
            wbuf[t] = weights
            return
        to_txt = dot(weights, img, 0, 0).reshape(TILE, NC, slots, emb_w)
        gtxt[at_txt] = gtxt[at_txt] + to_txt if t in begun_txt else to_txt
        begun_txt.add(t)

    begun_img, begun_txt = set(), set()

    def ring_sum(p):
        k = most_up + 2 - 2 * p
        for h in range(ZCH):
            rows = pl.ds(h * zrows, zrows)
            total = None
            for sign, most, got, sems in ways(h, rs_up, rs_dn, zr_up, zr_dn):
                if k <= most:
                    here = spot(sign * k)
                    if total is None or k:
                        total = gimg[here, rows]
                    for far in (k + 1, k + 2):
                        if far <= most:
                            arrived(got.at[far - 1, rows], sems.at[far - 1, h])
                            total = total + got[far - 1, rows].astype(f32)
                    if k:
                        rs_out[here, rows] = total.astype(bf16)
                        send(rs_out.at[here, rows], got.at[k - 1, rows],
                             sems.at[k - 1, h], at(dz=2 * sign))
                if 1 <= k - 1 <= most:
                    here = spot(sign * (k - 1))
                    rs_out[here, rows] = gimg[here, rows].astype(bf16)
                    send(rs_out.at[here, rows], got.at[k - 2, rows],
                         sems.at[k - 2, h], at(dz=sign))
            if k == 0:
                gimg[0, rows] = total

    def core_send(t):
        part = pl.ds(t * TILE, TILE)
        send(gtxt.at[part, 1], rcore.at[part], cr_sem.at[t], at(dc=1))

    def plane_send(t):
        part = pl.ds(t * TILE, TILE)
        arrived(rcore.at[part], cr_sem.at[t])
        for n in range(t * TILE, (t + 1) * TILE):
            both = gtxt[n, 0] + rcore[n]
            if n == 0:
                gtxt[0, 0] = both
            else:
                sbuf[n] = both.astype(sbuf.dtype)
                dx, dy = order[n]
                send(sbuf.at[n], rxy.at[n], xr_sem.at[n - 1], at(dx=-dx, dy=-dy))

    def finish(side, total, emb, other):
        own = temper_val * jnp.sum(emb * other, axis=1, keepdims=True) + bias_val
        own = (-1.0 / (1.0 + jnp.exp(own))).astype(bf16).astype(f32)
        grad = jnp.where(live, factor * (total + own * other), 0.0)
        inner = sum(
            jnp.sum(unit[side * ny + k] * grad[:, k * col_w:(k + 1) * col_w],
                    axis=1, keepdims=True)
            for k in range(ny)
        )
        for k in range(ny):
            part = grad[:, k * col_w:(k + 1) * col_w]
            gp[side * ny + k] = (
                norm[side] * (part - unit[side * ny + k] * inner)
            ).astype(bf16)
        for dy in (2, 1, 3):
            if dy < ny:
                send(gp.at[side * ny + (y + dy) % ny], gpr.at[side * ny + y],
                     yb_sem.at[side, dy - 1], at(dy=dy))
        gpr[side * ny + y] = gp[side * ny + y]

    def weight_grad(side):
        for dy in range(1, ny):
            arrived(gpr.at[side * ny + (y - dy + ny) % ny], yb_sem.at[side, dy - 1])
        grad = gpr[side * ny:(side + 1) * ny].reshape(ny * slots, col_w)
        gw[side] = dot(feats_t[side], grad).reshape(gw.shape[1:])
        send(gw.at[side, :, :, 1 - c], gwc.at[side], fc_sem.at[side], at(dc=1))

    far_first = sorted(range(nz), key=lambda d: -min(d, nz - d))
    per = nz // PARTS

    def over_x(side):
        arrived(gwc.at[side], fc_sem.at[side])
        for part in range(PARTS):
            piece = pl.ds(part * per, per)
            for n in range(part * per, (part + 1) * per):
                there = (z + far_first[n]) % nz
                gx[side, n] = gw[side, there, :, c] + gwc[side, there]
            for dx in (2, 1, 3):
                if dx < NX:
                    send(gx.at[side, piece, (x + dx) % NX], gxr.at[side, dx - 1, piece],
                         fx_sem.at[side, dx - 1, part], at(dx=dx))

    def over_z(side):
        for part in range(PARTS):
            piece = pl.ds(part * per, per)
            total = gx[side, piece, x]
            for dx in range(1, NX):
                arrived(gxr.at[side, dx - 1, piece], fx_sem.at[side, dx - 1, part])
                total = total + gxr[side, dx - 1, piece]
            gz[side, piece] = total
            for n in range(part * per, min((part + 1) * per, nz - 1)):
                send(gz.at[side, n], gzr.at[side, n], fz_sem.at[side, n], at(dz=far_first[n]))

    def collect(side, out):
        total = gz[side, nz - 1]
        for n in range(nz - 1):
            arrived(gzr.at[side, n], fz_sem.at[side, n])
            total = total + gzr[side, n]
        out[...] = total

    project(0)
    temper_val, bias_val = temper[0], bias[0]
    factor = loss_scale[0] * temper_val / (LRN * nz * NX * NC)
    slot_at = y * slots + lax.broadcasted_iota(jnp.int32, (slots, 1), 0)
    live = slot_at < cnt[0]
    pl.semaphore_wait(barrier, len(partners))
    deal(0)
    project(1)
    deal(1)
    embed(0)
    ring_send(1)
    embed(1)
    spread()
    for side in range(2):
        feats_t[side] = feats[side].T

    for p in range(2, most_up // 2 + 2):
        ring_send(p)
        ring_odd(p - 1)
        for what, *which in PLAN[p]:
            {"hand": hand_over, "ready": tile_ready, "pair": pair_tile}[what](*which)
    for t in range(tiles):
        pair_tile(groups - 1, t, "img")
    ring_sum(1)
    for t in range(tiles - 1):
        pair_tile(groups - 1, t, "txt")
        core_send(t)
    for g in range(groups - 2, -1, -1):
        pair_tile(g, tiles - 1)
    pair_tile(groups - 1, tiles - 1, "txt")
    core_send(tiles - 1)
    done = 0
    for p in range(2, most_up // 2 + 1):
        for t in range(done, min(done + 2, tiles)):
            plane_send(t)
        done = min(done + 2, tiles)
        ring_sum(p)
    for t in range(done, tiles):
        plane_send(t)
    emb_i = zbuf[0].astype(f32)
    emb_t = pbuf[0, 0].astype(f32)
    for n in range(1, len(order)):
        arrived(rxy.at[n], xr_sem.at[n - 1])
    total = gtxt[0, 0]
    for n in range(1, len(order)):
        total = total + rxy[n].astype(f32)
    finish(1, total, emb_t, emb_i)
    ring_sum(most_up // 2 + 1)
    finish(0, gimg[0], emb_i, emb_t)
    weight_grad(1)
    over_x(1)
    weight_grad(0)
    over_x(0)
    over_z(1)
    over_z(0)
    collect(1, out_txt)
    collect(0, out_img)
    for copy in sends:
        copy.wait_send()


def on_device(
    pool_img, pool_txt, w_img, w_txt, logit_scale, logit_bias, loss_scale, select, counts
):
    ny = lax.axis_size("tower")
    rows_n = lax.axis_size("rows")
    nz = rows_n // (NX * NC)
    chips = NX * ny
    list_len = select.shape[0]
    slots = list_len // ny
    depth, col_w = w_img.shape
    emb_w = col_w * ny
    out_rows = depth // rows_n
    most_up = nz // 2
    vmem = pltpu.VMEM
    dma = pltpu.SemaphoreType.DMA
    out = jax.ShapeDtypeStruct((out_rows, col_w), f32)
    scratch = [
        vmem((2,) + pool_img.shape, bf16),
        vmem((2, depth, col_w), bf16),
        vmem((list_len,), jnp.int32),
        vmem((2, list_len, depth), bf16),
        vmem((2, depth, list_len), bf16),
        vmem((2, list_len, col_w), f32),
        vmem((2 * ny, slots, col_w), f32),
        vmem((2, slots, 1), f32),
        vmem((nz, slots, emb_w), bf16),
        vmem((chips, NC, slots, emb_w), bf16),
        vmem((nz, slots, emb_w), f32),
        vmem((chips, NC, slots, emb_w), f32),
        vmem((chips // TILE, (GROUPS[-1] - GROUPS[-2]) * slots, TILE * NC * slots), bf16),
        vmem((nz, slots, emb_w), bf16),
        vmem((most_up, slots, emb_w), bf16),
        vmem((most_up, slots, emb_w), bf16),
        vmem((chips, slots, emb_w), f32),
        vmem((chips, slots, emb_w), bf16),
        vmem((chips, slots, emb_w), bf16),
        vmem((2 * ny, slots, col_w), bf16),
        vmem((2 * ny, slots, col_w), bf16),
        vmem((2, nz, NX, NC, out_rows, col_w), f32),
        vmem((2, nz, NX, out_rows, col_w), f32),
        vmem((2, nz, NX, out_rows, col_w), f32),
        vmem((2, NX - 1, nz, out_rows, col_w), f32),
        vmem((2, nz, out_rows, col_w), f32),
        vmem((2, nz - 1, out_rows, col_w), f32),
        dma((5,)),
        dma((2, ny - 1, 2)),
        dma((most_up, ZCH, 2)),
        dma((most_up, ZCH, 2)),
        dma((chips - 1, 2)),
        dma((chips, 2)),
        dma((most_up, ZCH, 2)),
        dma((most_up, ZCH, 2)),
        dma((chips // TILE, 2)),
        dma((chips - 1, 2)),
        dma((2, ny - 1, 2)),
        dma((2, 2)),
        dma((2, NX - 1, PARTS, 2)),
        dma((2, nz - 1, 2)),
    ]
    whole = pl.BlockSpec(memory_space=vmem)
    placed = pl.BlockSpec(memory_space=pl.ANY)
    step = pl.pallas_call(
        functools.partial(kernel, (nz, ny)),
        out_shape=(out, out),
        in_specs=[placed] * 5 + [pl.BlockSpec(memory_space=pltpu.SMEM)] * 4,
        out_specs=(whole, whole),
        scratch_shapes=scratch,
        compiler_params=pltpu.CompilerParams(
            collective_id=0, has_side_effects=True, vmem_limit_bytes=60 << 20
        ),
        name="learner_step",
    )(
        pool_img, pool_txt, w_img, w_txt, select, counts,
        logit_scale, logit_bias, loss_scale,
    )
    return pl.pallas_call(
        hand_out, out_shape=(out, out), in_specs=[whole] * 2, out_specs=(whole, whole),
        name="hand_out",
    )(*step)


def hand_out(img, txt, out_img, out_txt):
    out_img[...] = img[...]
    out_txt[...] = txt[...]


def solution(mesh):
    in_specs = (
        P("rows", None),
        P("rows", None),
        P(None, "tower"),
        P(None, "tower"),
        P(),
        P(),
        P(),
        P("rows"),
        P("rows"),
    )
    out_specs = (P("rows", "tower"), P("rows", "tower"))
    return jax.shard_map(
        on_device, mesh=mesh, in_specs=in_specs, out_specs=out_specs, check_vma=False
    )
```

```python
import functools

import jax
import jax.numpy as jnp
from jax import lax
from jax.experimental import pallas as pl
from jax.experimental.pallas import tpu as pltpu
from jax.sharding import PartitionSpec as P

bf16 = jnp.bfloat16
f32 = jnp.float32
eps = 1e-06

NX, NC = 4, 2
LRN = 128
PLAN = {
    2: [("hand", 0)],
    3: [("hand", 1), ("ready", 0), ("pair", 0, 0), ("pair", 1, 0),
        ("ready", 1), ("pair", 0, 1), ("pair", 1, 1), ("hand", 2)],
    4: [("hand", 3), ("pair", 2, 0), ("pair", 2, 1),
        ("ready", 2), ("pair", 0, 2), ("pair", 1, 2), ("pair", 2, 2)],
    5: [("ready", 3)],
}
GROUPS, TILE = (0, 5, 9, 13, 16), 4
ZCH = 2
PARTS = 4
NEAR_Z = 2


def dot(a, b, ca=1, cb=0):
    return lax.dot_general(a, b, (((ca,), (cb,)), ((), ())), preferred_element_type=f32)


def chip_order(nx, ny):
    ring = lambda d, n: min(d, n - d)
    places = [(dx, dy) for dx in range(nx) for dy in range(ny)]
    return sorted(places, key=lambda p: (ring(p[0], nx) + ring(p[1], ny), p))


def kernel(
    cfg,
    h_pool_img, h_pool_txt, h_w_img, h_w_txt, h_sel, cnt, temper, bias, loss_scale,
    out_img, out_txt,
    pool, w, sel,
    feats, ft, fh, fh_send, proj, unit, norm, zbuf, pbuf, gimg, gtxt, wbuf, rs_out, rs_up, rs_dn,
    rcore, sbuf, rxy, gp, gpr, gw, gx, gxr, gz, gzr,
    in_sem, y_sem, za_up, za_dn, xy_sem, cf_sem, zr_up, zr_dn, cr_sem, xr_sem, yb_sem,
    fh_sem, fx_sem, fz_sem,
):
    nz, ny = cfg
    row, y = lax.axis_index("rows"), lax.axis_index("tower")
    c = row % NC
    x = row // NC % NX
    z = row // (NC * NX)
    most_up = nz // 2
    order = chip_order(NX, ny)
    groups, tiles = len(GROUPS) - 1, len(order) // TILE
    slots = unit.shape[1]
    emb_w = zbuf.shape[2]
    col_w = proj.shape[2]
    sends = []

    def at(dz=0, dx=0, dy=0, dc=0):
        r = ((z + dz + nz) % nz * NX + (x + dx + NX) % NX) * NC + (c + dc) % NC
        return (r, (y + dy + ny) % ny)

    def send(src, dst, sems, where):
        copy = pltpu.make_async_remote_copy(
            src_ref=src, dst_ref=dst, send_sem=sems.at[0], recv_sem=sems.at[1],
            device_id=where, device_id_type=pl.DeviceIdType.MESH,
        )
        copy.start()
        sends.append(copy)

    def arrived(ref, sems):
        pltpu.make_async_remote_copy(
            src_ref=ref, dst_ref=ref, send_sem=sems.at[0], recv_sem=sems.at[1],
            device_id=at(), device_id_type=pl.DeviceIdType.MESH,
        ).wait_recv()

    loads = [
        pltpu.make_async_copy(src, dst, in_sem.at[n])
        for n, (src, dst) in enumerate((
            (h_sel, sel), (h_pool_img, pool.at[0]), (h_w_img, w.at[0]),
            (h_pool_txt, pool.at[1]), (h_w_txt, w.at[1]),
        ))
    ]
    for load in loads:
        load.start()
    partners = [at(dx=dx, dy=dy) for dx, dy in order[1:]]
    partners += [at(dz=dz) for dz in [d for d in range(1, nz) if min(d, nz - d) <= NEAR_Z]] + [at(dc=1)]
    partners += [at(dy=dy, dc=1) for dy in range(1, ny)]
    barrier = pltpu.get_barrier_semaphore()
    for there in partners:
        pl.semaphore_signal(
            barrier, inc=1, device_id=there, device_id_type=pl.DeviceIdType.MESH
        )

    loads[0].wait()
    rows_at = lax.broadcasted_iota(jnp.int32, (pool.shape[1], sel.shape[0]), 0)
    pick = jnp.where(sel[...][None, :] == rows_at, 1.0, 0.0).astype(bf16)

    def project(side):
        loads[1 + 2 * side].wait()
        feats[side] = dot(pick, pool[side], 0, 0).astype(bf16)
        loads[2 + 2 * side].wait()
        proj[side] = dot(feats[side], w[side])

    def deal(side):
        for dy in (2, 1, 3):
            if dy >= ny:
                continue
            yy = (y + dy) % ny
            send(
                proj.at[side, pl.ds(pl.multiple_of(yy * slots, slots), slots)],
                unit.at[side * ny + y], y_sem.at[side, dy - 1], at(dy=dy),
            )
        unit[side * ny + y] = proj[side, pl.ds(pl.multiple_of(y * slots, slots), slots)]

    def embed(side):
        for dy in range(1, ny):
            arrived(unit.at[side * ny + (y - dy + ny) % ny], y_sem.at[side, dy - 1])
        parts = [unit[side * ny + k] for k in range(ny)]
        square = sum(jnp.sum(part * part, axis=1, keepdims=True) for part in parts)
        norm[side] = lax.rsqrt(square + eps)
        for k in range(ny):
            rows = parts[k] * norm[side]
            unit[side * ny + k] = rows
            emb = jnp.where(live, rows, 0.0).astype(bf16)
            if side == 0:
                zbuf[0, :, k * col_w:(k + 1) * col_w] = emb
            else:
                pbuf[0, 0, :, k * col_w:(k + 1) * col_w] = emb

    def spot(offset):
        return 2 * offset if 0 <= offset < most_up else 2 * abs(offset) - 1

    zrows = slots // ZCH

    def ways(h, *args):
        up = h < ZCH // 2
        return [
            (1, most_up - (not up), *args[0::2]), (-1, most_up - up, *args[1::2])
        ]

    def ring_send(p):
        k = 2 * p - 2
        for h in range(ZCH):
            rows = pl.ds(h * zrows, zrows)
            for sign, most, sems in ways(h, za_up, za_dn):
                if k > most:
                    continue
                have = zbuf.at[spot(-sign * k), rows]
                if k:
                    arrived(have, sems.at[k - 1, h])
                for step in (2, 1):
                    if k + step <= most:
                        send(have, zbuf.at[spot(-sign * (k + step)), rows],
                             sems.at[k + step - 1, h], at(dz=sign * step))

    def ring_odd(p):
        k = 2 * p - 1
        for h in range(ZCH):
            rows = pl.ds(h * zrows, zrows)
            for sign, most, sems in ways(h, za_up, za_dn):
                if k <= most:
                    arrived(zbuf.at[spot(-sign * k), rows], sems.at[k - 1, h])

    def spread():
        for n, (dx, dy) in enumerate(order[1:]):
            send(pbuf.at[0, 0], pbuf.at[n + 1, 0], xy_sem.at[n], at(dx=dx, dy=dy))
        send(pbuf.at[0, 0], pbuf.at[0, 1], cf_sem.at[0], at(dc=1))

    def hand_over(t):
        for n in range(t * TILE, (t + 1) * TILE):
            if n:
                arrived(pbuf.at[n, 0], xy_sem.at[n - 1])
                send(pbuf.at[n, 0], pbuf.at[n, 1], cf_sem.at[n], at(dc=1))

    def tile_ready(t):
        for n in range(t * TILE, (t + 1) * TILE):
            arrived(pbuf.at[n, 1], cf_sem.at[n])

    def pair_tile(g, t, part=None):
        at_img = slice(GROUPS[g], GROUPS[g + 1])
        count = GROUPS[g + 1] - GROUPS[g]
        img = zbuf[at_img].reshape(count * slots, emb_w)
        txt = pbuf[t * TILE:(t + 1) * TILE].reshape(TILE * NC * slots, emb_w)
        at_txt = slice(t * TILE, (t + 1) * TILE)
        if part == "txt":
            to_txt = dot(wbuf[t], img, 0, 0).reshape(TILE, NC, slots, emb_w)
            gtxt[at_txt] = gtxt[at_txt] + to_txt
            return
        logits = temper_val * dot(img, txt, 1, 1) + bias_val
        weights = 1.0 / (1.0 + jnp.exp(-logits))
        if g == 0 and t == 0:
            i = lax.broadcasted_iota(jnp.int32, logits.shape, 0)
            j = lax.broadcasted_iota(jnp.int32, logits.shape, 1)
            weights = jnp.where((i == j) & (i < slots), 0.0, weights)
        weights = weights.astype(bf16)
        to_img = dot(weights, txt).reshape(count, slots, emb_w)
        gimg[at_img] = gimg[at_img] + to_img if g in begun_img else to_img
        begun_img.add(g)
        if part == "img":
            wbuf[t] = weights
            return
        to_txt = dot(weights, img, 0, 0).reshape(TILE, NC, slots, emb_w)
        gtxt[at_txt] = gtxt[at_txt] + to_txt if t in begun_txt else to_txt
        begun_txt.add(t)

    begun_img, begun_txt = set(), set()

    def ring_sum(p):
        k = most_up + 2 - 2 * p
        for h in range(ZCH):
            rows = pl.ds(h * zrows, zrows)
            total = None
            for sign, most, got, sems in ways(h, rs_up, rs_dn, zr_up, zr_dn):
                if k <= most:
                    here = spot(sign * k)
                    if total is None or k:
                        total = gimg[here, rows]
                    for far in (k + 1, k + 2):
                        if far <= most:
                            arrived(got.at[far - 1, rows], sems.at[far - 1, h])
                            total = total + got[far - 1, rows].astype(f32)
                    if k:
                        rs_out[here, rows] = total.astype(bf16)
                        send(rs_out.at[here, rows], got.at[k - 1, rows],
                             sems.at[k - 1, h], at(dz=2 * sign))
                if 1 <= k - 1 <= most:
                    here = spot(sign * (k - 1))
                    rs_out[here, rows] = gimg[here, rows].astype(bf16)
                    send(rs_out.at[here, rows], got.at[k - 2, rows],
                         sems.at[k - 2, h], at(dz=sign))
            if k == 0:
                gimg[0, rows] = total

    def core_send(t):
        part = pl.ds(t * TILE, TILE)
        send(gtxt.at[part, 1], rcore.at[part], cr_sem.at[t], at(dc=1))

    def plane_send(t):
        part = pl.ds(t * TILE, TILE)
        arrived(rcore.at[part], cr_sem.at[t])
        for n in range(t * TILE, (t + 1) * TILE):
            both = gtxt[n, 0] + rcore[n]
            if n == 0:
                gtxt[0, 0] = both
            else:
                sbuf[n] = both.astype(sbuf.dtype)
                dx, dy = order[n]
                send(sbuf.at[n], rxy.at[n], xr_sem.at[n - 1], at(dx=-dx, dy=-dy))

    def finish(side, total, emb, other):
        own = temper_val * jnp.sum(emb * other, axis=1, keepdims=True) + bias_val
        own = (-1.0 / (1.0 + jnp.exp(own))).astype(bf16).astype(f32)
        grad = jnp.where(live, factor * (total + own * other), 0.0)
        inner = sum(
            jnp.sum(unit[side * ny + k] * grad[:, k * col_w:(k + 1) * col_w],
                    axis=1, keepdims=True)
            for k in range(ny)
        )
        for k in range(ny):
            part = grad[:, k * col_w:(k + 1) * col_w]
            gp[side * ny + k] = (
                norm[side] * (part - unit[side * ny + k] * inner)
            ).astype(bf16)
        for dy in (2, 1, 3, 0):
            for dc in range(NC):
                if dy < ny and (dy or dc):
                    send(gp.at[side * ny + (y + dy) % ny], gpr.at[(side * NC + dc) * ny + y],
                         yb_sem.at[side, dc, dy], at(dy=dy, dc=dc))
        gpr[side * NC * ny + y] = gp[side * ny + y]

    def weight_grad(side):
        arrived(fh.at[side, 1], fh_sem.at[side])
        total = None
        for dc in range(NC):
            first = (side * NC + dc) * ny
            for dy in range(ny):
                if dy or dc:
                    arrived(gpr.at[first + (y - dy + ny) % ny], yb_sem.at[side, dc, dy])
            part = dot(fh[side, dc], gpr[first:first + ny].reshape(ny * slots, col_w))
            total = part if total is None else total + part
        gw[side] = total.reshape(gw.shape[1:])

    far_first = sorted(range(nz), key=lambda d: -min(d, nz - d))
    per = nz // PARTS

    def over_x(side):
        for part in range(PARTS):
            piece = pl.ds(part * per, per)
            for n in range(part * per, (part + 1) * per):
                gx[side, n] = gw[side, (z + far_first[n]) % nz]
            for dx in (2, 1, 3):
                if dx < NX:
                    send(gx.at[side, piece, (x + dx) % NX], gxr.at[side, dx - 1, piece],
                         fx_sem.at[side, dx - 1, part], at(dx=dx))

    def over_z(side):
        for part in range(PARTS):
            piece = pl.ds(part * per, per)
            total = gx[side, piece, x]
            for dx in range(1, NX):
                arrived(gxr.at[side, dx - 1, piece], fx_sem.at[side, dx - 1, part])
                total = total + gxr[side, dx - 1, piece]
            gz[side, piece] = total
            for n in range(part * per, min((part + 1) * per, nz - 1)):
                send(gz.at[side, n], gzr.at[side, n], fz_sem.at[side, n], at(dz=far_first[n]))

    def collect(side, out):
        total = gz[side, nz - 1]
        for n in range(nz - 1):
            arrived(gzr.at[side, n], fz_sem.at[side, n])
            total = total + gzr[side, n]
        out[...] = total

    project(0)
    temper_val, bias_val = temper[0], bias[0]
    factor = loss_scale[0] * temper_val / (LRN * nz * NX * NC)
    slot_at = y * slots + lax.broadcasted_iota(jnp.int32, (slots, 1), 0)
    live = slot_at < cnt[0]
    pl.semaphore_wait(barrier, len(partners))
    deal(0)
    project(1)
    deal(1)
    embed(0)
    ring_send(1)
    embed(1)
    spread()
    for side in range(2):
        ft[...] = feats[side].T.astype(f32).reshape(ft.shape)
        fh[side, 0] = ft[:, :, c].reshape(fh.shape[2:]).astype(bf16)
        fh_send[side] = ft[:, :, 1 - c].reshape(fh.shape[2:]).astype(bf16)
        send(fh_send.at[side], fh.at[side, 1], fh_sem.at[side], at(dc=1))

    for p in range(2, most_up // 2 + 2):
        ring_send(p)
        ring_odd(p - 1)
        for what, *which in PLAN[p]:
            {"hand": hand_over, "ready": tile_ready, "pair": pair_tile}[what](*which)
    for t in range(tiles):
        pair_tile(groups - 1, t, "img")
    ring_sum(1)
    for t in range(tiles - 1):
        pair_tile(groups - 1, t, "txt")
        core_send(t)
    for g in range(groups - 2, -1, -1):
        pair_tile(g, tiles - 1)
    pair_tile(groups - 1, tiles - 1, "txt")
    core_send(tiles - 1)
    done = 0
    for p in range(2, most_up // 2 + 1):
        for t in range(done, min(done + 2, tiles)):
            plane_send(t)
        done = min(done + 2, tiles)
        ring_sum(p)
    for t in range(done, tiles):
        plane_send(t)
    emb_i = zbuf[0].astype(f32)
    emb_t = pbuf[0, 0].astype(f32)
    for n in range(1, len(order)):
        arrived(rxy.at[n], xr_sem.at[n - 1])
    total = gtxt[0, 0]
    for n in range(1, len(order)):
        total = total + rxy[n].astype(f32)
    finish(1, total, emb_t, emb_i)
    ring_sum(most_up // 2 + 1)
    finish(0, gimg[0], emb_i, emb_t)
    weight_grad(1)
    over_x(1)
    weight_grad(0)
    over_x(0)
    over_z(1)
    over_z(0)
    collect(1, out_txt)
    collect(0, out_img)
    for copy in sends:
        copy.wait_send()


def on_device(
    pool_img, pool_txt, w_img, w_txt, logit_scale, logit_bias, loss_scale, select, counts
):
    ny = lax.axis_size("tower")
    rows_n = lax.axis_size("rows")
    nz = rows_n // (NX * NC)
    chips = NX * ny
    list_len = select.shape[0]
    slots = list_len // ny
    depth, col_w = w_img.shape
    emb_w = col_w * ny
    out_rows = depth // rows_n
    most_up = nz // 2
    vmem = pltpu.VMEM
    dma = pltpu.SemaphoreType.DMA
    out = jax.ShapeDtypeStruct((out_rows, col_w), f32)
    scratch = [
        vmem((2,) + pool_img.shape, bf16),
        vmem((2, depth, col_w), bf16),
        vmem((list_len,), jnp.int32),
        vmem((2, list_len, depth), bf16),
        vmem((nz, NX, NC, out_rows, list_len), f32),
        vmem((2, NC, depth // NC, list_len), bf16),
        vmem((2, depth // NC, list_len), bf16),
        vmem((2, list_len, col_w), f32),
        vmem((2 * ny, slots, col_w), f32),
        vmem((2, slots, 1), f32),
        vmem((nz, slots, emb_w), bf16),
        vmem((chips, NC, slots, emb_w), bf16),
        vmem((nz, slots, emb_w), f32),
        vmem((chips, NC, slots, emb_w), f32),
        vmem((chips // TILE, (GROUPS[-1] - GROUPS[-2]) * slots, TILE * NC * slots), bf16),
        vmem((nz, slots, emb_w), bf16),
        vmem((most_up, slots, emb_w), bf16),
        vmem((most_up, slots, emb_w), bf16),
        vmem((chips, slots, emb_w), f32),
        vmem((chips, slots, emb_w), bf16),
        vmem((chips, slots, emb_w), bf16),
        vmem((2 * ny, slots, col_w), bf16),
        vmem((2 * NC * ny, slots, col_w), bf16),
        vmem((2, nz, NX, out_rows, col_w), f32),
        vmem((2, nz, NX, out_rows, col_w), f32),
        vmem((2, NX - 1, nz, out_rows, col_w), f32),
        vmem((2, nz, out_rows, col_w), f32),
        vmem((2, nz - 1, out_rows, col_w), f32),
        dma((5,)),
        dma((2, ny - 1, 2)),
        dma((most_up, ZCH, 2)),
        dma((most_up, ZCH, 2)),
        dma((chips - 1, 2)),
        dma((chips, 2)),
        dma((most_up, ZCH, 2)),
        dma((most_up, ZCH, 2)),
        dma((chips // TILE, 2)),
        dma((chips - 1, 2)),
        dma((2, NC, ny, 2)),
        dma((2, 2)),
        dma((2, NX - 1, PARTS, 2)),
        dma((2, nz - 1, 2)),
    ]
    whole = pl.BlockSpec(memory_space=vmem)
    placed = pl.BlockSpec(memory_space=pl.ANY)
    step = pl.pallas_call(
        functools.partial(kernel, (nz, ny)),
        out_shape=(out, out),
        in_specs=[placed] * 5 + [pl.BlockSpec(memory_space=pltpu.SMEM)] * 4,
        out_specs=(whole, whole),
        scratch_shapes=scratch,
        compiler_params=pltpu.CompilerParams(
            collective_id=0, has_side_effects=True, vmem_limit_bytes=60 << 20
        ),
        name="learner_step",
    )(
        pool_img, pool_txt, w_img, w_txt, select, counts,
        logit_scale, logit_bias, loss_scale,
    )
    return pl.pallas_call(
        hand_out, out_shape=(out, out), in_specs=[whole] * 2, out_specs=(whole, whole),
        name="hand_out",
    )(*step)


def hand_out(img, txt, out_img, out_txt):
    out_img[...] = img[...]
    out_txt[...] = txt[...]


def solution(mesh):
    in_specs = (
        P("rows", None),
        P("rows", None),
        P(None, "tower"),
        P(None, "tower"),
        P(),
        P(),
        P(),
        P("rows"),
        P("rows"),
    )
    out_specs = (P("rows", "tower"), P("rows", "tower"))
    return jax.shard_map(
        on_device, mesh=mesh, in_specs=in_specs, out_specs=out_specs, check_vma=False
    )
```

```python
import functools

import jax
import jax.numpy as jnp
from jax import lax
from jax.experimental import pallas as pl
from jax.experimental.pallas import tpu as pltpu
from jax.sharding import PartitionSpec as P

bf16 = jnp.bfloat16
f32 = jnp.float32
eps = 1e-06

NX, NC = 4, 2
LRN = 128
PLAN = {
    2: [("hand", 0)],
    3: [("hand", 1), ("ready", 0), ("pair", 0, 0), ("pair", 1, 0),
        ("ready", 1), ("pair", 0, 1), ("pair", 1, 1), ("hand", 2)],
    4: [("hand", 3), ("pair", 2, 0), ("pair", 2, 1),
        ("ready", 2), ("pair", 0, 2), ("pair", 1, 2), ("pair", 2, 2)],
    5: [("ready", 3)],
}
GROUPS, TILE = (0, 5, 9, 13, 16), 4
ZCH = 2
PARTS = 4
NEAR_Z = 2


def dot(a, b, ca=1, cb=0):
    return lax.dot_general(a, b, (((ca,), (cb,)), ((), ())), preferred_element_type=f32)


def chip_order(nx, ny):
    ring = lambda d, n: min(d, n - d)
    places = [(dx, dy) for dx in range(nx) for dy in range(ny)]
    return sorted(places, key=lambda p: (ring(p[0], nx) + ring(p[1], ny), p))


def kernel(
    cfg,
    h_pool_img, h_pool_txt, h_w_img, h_w_txt, h_sel, cnt, temper, bias, loss_scale,
    out_img, out_txt,
    pool, w, sel,
    feats, ft, fh, fh_send, proj, unit, norm, zbuf, pbuf, gimg, gtxt, wbuf, rs_out, rs_up, rs_dn,
    rcore, sbuf, rxy, gp, gpr, gw, gx, gxr, gz, gzr,
    in_sem, y_sem, za_up, za_dn, xy_sem, cf_sem, zr_up, zr_dn, cr_sem, xr_sem, yb_sem,
    fh_sem, fx_sem, fz_sem,
):
    nz, ny = cfg
    row, y = lax.axis_index("rows"), lax.axis_index("tower")
    c = row % NC
    x = row // NC % NX
    z = row // (NC * NX)
    most_up = nz // 2
    order = chip_order(NX, ny)
    groups, tiles = len(GROUPS) - 1, len(order) // TILE
    slots = unit.shape[1]
    emb_w = zbuf.shape[2]
    col_w = proj.shape[2]
    sends = []

    def at(dz=0, dx=0, dy=0, dc=0):
        r = ((z + dz + nz) % nz * NX + (x + dx + NX) % NX) * NC + (c + dc) % NC
        return (r, (y + dy + ny) % ny)

    def send(src, dst, sems, where):
        copy = pltpu.make_async_remote_copy(
            src_ref=src, dst_ref=dst, send_sem=sems.at[0], recv_sem=sems.at[1],
            device_id=where, device_id_type=pl.DeviceIdType.MESH,
        )
        copy.start()
        sends.append(copy)

    def arrived(ref, sems):
        pltpu.make_async_remote_copy(
            src_ref=ref, dst_ref=ref, send_sem=sems.at[0], recv_sem=sems.at[1],
            device_id=at(), device_id_type=pl.DeviceIdType.MESH,
        ).wait_recv()

    loads = [
        pltpu.make_async_copy(src, dst, in_sem.at[n])
        for n, (src, dst) in enumerate((
            (h_sel, sel), (h_pool_img, pool.at[0]), (h_w_img, w.at[0]),
            (h_pool_txt, pool.at[1]), (h_w_txt, w.at[1]),
        ))
    ]
    for load in loads:
        load.start()
    partners = [at(dx=dx, dy=dy) for dx, dy in order[1:]]
    partners += [at(dz=dz) for dz in [d for d in range(1, nz) if min(d, nz - d) <= NEAR_Z]] + [at(dc=1)]
    partners += [at(dy=dy, dc=1) for dy in range(1, ny)]
    barrier = pltpu.get_barrier_semaphore()
    for there in partners:
        pl.semaphore_signal(
            barrier, inc=1, device_id=there, device_id_type=pl.DeviceIdType.MESH
        )

    loads[0].wait()
    rows_at = lax.broadcasted_iota(jnp.int32, (pool.shape[1], sel.shape[0]), 0)
    pick = jnp.where(sel[...][None, :] == rows_at, 1.0, 0.0).astype(bf16)

    def project(side):
        loads[1 + 2 * side].wait()
        feats[side] = dot(pick, pool[side], 0, 0).astype(bf16)
        loads[2 + 2 * side].wait()
        proj[side] = dot(feats[side], w[side])

    def deal(side):
        for dy in (2, 1, 3):
            if dy >= ny:
                continue
            yy = (y + dy) % ny
            send(
                proj.at[side, pl.ds(pl.multiple_of(yy * slots, slots), slots)],
                unit.at[side * ny + y], y_sem.at[side, dy - 1], at(dy=dy),
            )
        unit[side * ny + y] = proj[side, pl.ds(pl.multiple_of(y * slots, slots), slots)]

    def embed(side):
        for dy in range(1, ny):
            arrived(unit.at[side * ny + (y - dy + ny) % ny], y_sem.at[side, dy - 1])
        parts = [unit[side * ny + k] for k in range(ny)]
        square = sum(jnp.sum(part * part, axis=1, keepdims=True) for part in parts)
        norm[side] = lax.rsqrt(square + eps)
        for k in range(ny):
            rows = parts[k] * norm[side]
            unit[side * ny + k] = rows
            emb = jnp.where(live, rows, 0.0).astype(bf16)
            if side == 0:
                zbuf[0, :, k * col_w:(k + 1) * col_w] = emb
            else:
                pbuf[0, 0, :, k * col_w:(k + 1) * col_w] = emb

    def spot(offset):
        return 2 * offset if 0 <= offset < most_up else 2 * abs(offset) - 1

    zrows = slots // ZCH

    def ways(h, *args):
        up = h < ZCH // 2
        return [
            (1, most_up - (not up), *args[0::2]), (-1, most_up - up, *args[1::2])
        ]

    def ring_send(p):
        k = 2 * p - 2
        for h in range(ZCH):
            rows = pl.ds(h * zrows, zrows)
            for sign, most, sems in ways(h, za_up, za_dn):
                if k > most:
                    continue
                have = zbuf.at[spot(-sign * k), rows]
                if k:
                    arrived(have, sems.at[k - 1, h])
                for step in (2, 1):
                    if k + step <= most:
                        send(have, zbuf.at[spot(-sign * (k + step)), rows],
                             sems.at[k + step - 1, h], at(dz=sign * step))

    def ring_odd(p):
        k = 2 * p - 1
        for h in range(ZCH):
            rows = pl.ds(h * zrows, zrows)
            for sign, most, sems in ways(h, za_up, za_dn):
                if k <= most:
                    arrived(zbuf.at[spot(-sign * k), rows], sems.at[k - 1, h])

    def spread():
        for n, (dx, dy) in enumerate(order[1:]):
            send(pbuf.at[0, 0], pbuf.at[n + 1, 0], xy_sem.at[n], at(dx=dx, dy=dy))
        send(pbuf.at[0, 0], pbuf.at[0, 1], cf_sem.at[0], at(dc=1))

    def hand_over(t):
        for n in range(t * TILE, (t + 1) * TILE):
            if n:
                arrived(pbuf.at[n, 0], xy_sem.at[n - 1])
                send(pbuf.at[n, 0], pbuf.at[n, 1], cf_sem.at[n], at(dc=1))

    def tile_ready(t):
        for n in range(t * TILE, (t + 1) * TILE):
            arrived(pbuf.at[n, 1], cf_sem.at[n])

    def pair_tile(g, t, part=None):
        at_img = slice(GROUPS[g], GROUPS[g + 1])
        count = GROUPS[g + 1] - GROUPS[g]
        img = zbuf[at_img].reshape(count * slots, emb_w)
        txt = pbuf[t * TILE:(t + 1) * TILE].reshape(TILE * NC * slots, emb_w)
        at_txt = slice(t * TILE, (t + 1) * TILE)
        if part == "txt":
            to_txt = dot(wbuf[t], img, 0, 0).reshape(TILE, NC, slots, emb_w)
            gtxt[at_txt] = gtxt[at_txt] + to_txt
            return
        logits = temper_val * dot(img, txt, 1, 1) + bias_val
        weights = 1.0 / (1.0 + jnp.exp(-logits))
        if g == 0 and t == 0:
            i = lax.broadcasted_iota(jnp.int32, logits.shape, 0)
            j = lax.broadcasted_iota(jnp.int32, logits.shape, 1)
            weights = jnp.where((i == j) & (i < slots), 0.0, weights)
        weights = weights.astype(bf16)
        to_img = dot(weights, txt).reshape(count, slots, emb_w)
        gimg[at_img] = gimg[at_img] + to_img if g in begun_img else to_img
        begun_img.add(g)
        if part == "img":
            wbuf[t] = weights
            return
        to_txt = dot(weights, img, 0, 0).reshape(TILE, NC, slots, emb_w)
        gtxt[at_txt] = gtxt[at_txt] + to_txt if t in begun_txt else to_txt
        begun_txt.add(t)

    begun_img, begun_txt = set(), set()

    def ring_sum(p):
        k = most_up + 2 - 2 * p
        for h in range(ZCH):
            rows = pl.ds(h * zrows, zrows)
            total = None
            for sign, most, got, sems in ways(h, rs_up, rs_dn, zr_up, zr_dn):
                if k <= most:
                    here = spot(sign * k)
                    if total is None or k:
                        total = gimg[here, rows]
                    for far in (k + 1, k + 2):
                        if far <= most:
                            arrived(got.at[far - 1, rows], sems.at[far - 1, h])
                            total = total + got[far - 1, rows].astype(f32)
                    if k:
                        rs_out[here, rows] = total.astype(bf16)
                        send(rs_out.at[here, rows], got.at[k - 1, rows],
                             sems.at[k - 1, h], at(dz=2 * sign))
                if 1 <= k - 1 <= most:
                    here = spot(sign * (k - 1))
                    rs_out[here, rows] = gimg[here, rows].astype(bf16)
                    send(rs_out.at[here, rows], got.at[k - 2, rows],
                         sems.at[k - 2, h], at(dz=sign))
            if k == 0:
                gimg[0, rows] = total

    def core_send(t):
        part = pl.ds(t * TILE, TILE)
        send(gtxt.at[part, 1], rcore.at[part], cr_sem.at[t], at(dc=1))

    def plane_send(t):
        part = pl.ds(t * TILE, TILE)
        arrived(rcore.at[part], cr_sem.at[t])
        for n in range(t * TILE, (t + 1) * TILE):
            both = gtxt[n, 0] + rcore[n]
            if n == 0:
                gtxt[0, 0] = both
            else:
                sbuf[n] = both.astype(sbuf.dtype)
                dx, dy = order[n]
                send(sbuf.at[n], rxy.at[n], xr_sem.at[n - 1], at(dx=-dx, dy=-dy))

    def finish(side, total, emb, other):
        own = temper_val * jnp.sum(emb * other, axis=1, keepdims=True) + bias_val
        own = (-1.0 / (1.0 + jnp.exp(own))).astype(bf16).astype(f32)
        grad = jnp.where(live, factor * (total + own * other), 0.0)
        inner = sum(
            jnp.sum(unit[side * ny + k] * grad[:, k * col_w:(k + 1) * col_w],
                    axis=1, keepdims=True)
            for k in range(ny)
        )
        for k in range(ny):
            part = grad[:, k * col_w:(k + 1) * col_w]
            gp[side * ny + k] = (
                norm[side] * (part - unit[side * ny + k] * inner)
            ).astype(bf16)
        for dy in (2, 1, 3, 0):
            for dc in range(NC):
                if dy < ny and (dy or dc):
                    send(gp.at[side * ny + (y + dy) % ny], gpr.at[(side * NC + dc) * ny + y],
                         yb_sem.at[side, dc, dy], at(dy=dy, dc=dc))
        gpr[side * NC * ny + y] = gp[side * ny + y]

    def weight_grad(side):
        arrived(fh.at[side, 1], fh_sem.at[side])
        total = None
        for dc in range(NC):
            first = (side * NC + dc) * ny
            for dy in range(ny):
                if dy or dc:
                    arrived(gpr.at[first + (y - dy + ny) % ny], yb_sem.at[side, dc, dy])
            part = dot(fh[side, dc], gpr[first:first + ny].reshape(ny * slots, col_w))
            total = part if total is None else total + part
        gw[side] = total.reshape(gw.shape[1:])

    far_first = sorted(range(nz), key=lambda d: -min(d, nz - d))
    per = nz // PARTS

    def over_x(side):
        for part in range(PARTS):
            piece = pl.ds(part * per, per)
            for n in range(part * per, (part + 1) * per):
                gx[side, n] = gw[side, (z + far_first[n]) % nz]
            for dx in (2, 1, 3):
                if dx < NX:
                    send(gx.at[side, piece, (x + dx) % NX], gxr.at[side, dx - 1, piece],
                         fx_sem.at[side, dx - 1, part], at(dx=dx))

    def over_z(side):
        for part in range(PARTS):
            piece = pl.ds(part * per, per)
            total = gx[side, piece, x]
            for dx in range(1, NX):
                arrived(gxr.at[side, dx - 1, piece], fx_sem.at[side, dx - 1, part])
                total = total + gxr[side, dx - 1, piece]
            gz[side, piece] = total
            for n in range(part * per, min((part + 1) * per, nz - 1)):
                send(gz.at[side, n], gzr.at[side, n], fz_sem.at[side, n], at(dz=far_first[n]))

    def collect(side, out):
        total = gz[side, nz - 1]
        for n in range(nz - 1):
            arrived(gzr.at[side, n], fz_sem.at[side, n])
            total = total + gzr[side, n]
        out[...] = total

    project(0)
    temper_val, bias_val = temper[0], bias[0]
    factor = loss_scale[0] * temper_val / (LRN * nz * NX * NC)
    slot_at = y * slots + lax.broadcasted_iota(jnp.int32, (slots, 1), 0)
    live = slot_at < cnt[0]
    pl.semaphore_wait(barrier, len(partners))
    deal(0)
    project(1)
    deal(1)
    embed(0)
    ring_send(1)
    embed(1)
    spread()
    for side in range(2):
        ft[...] = feats[side].T.astype(f32).reshape(ft.shape)
        fh[side, 0] = ft[:, :, c].reshape(fh.shape[2:]).astype(bf16)
        fh_send[side] = ft[:, :, 1 - c].reshape(fh.shape[2:]).astype(bf16)
        send(fh_send.at[side], fh.at[side, 1], fh_sem.at[side], at(dc=1))

    for p in range(2, most_up // 2 + 2):
        ring_send(p)
        ring_odd(p - 1)
        for what, *which in PLAN[p]:
            {"hand": hand_over, "ready": tile_ready, "pair": pair_tile}[what](*which)
    for t in range(tiles):
        pair_tile(groups - 1, t, "img")
    ring_sum(1)
    for t in range(tiles - 1):
        pair_tile(groups - 1, t, "txt")
        core_send(t)
    for g in range(groups - 2, -1, -1):
        pair_tile(g, tiles - 1)
    pair_tile(groups - 1, tiles - 1, "txt")
    core_send(tiles - 1)
    done = 0
    for p in range(2, most_up // 2 + 1):
        for t in range(done, min(done + 3, tiles)):
            plane_send(t)
        done = min(done + 3, tiles)
        ring_sum(p)
    for t in range(done, tiles):
        plane_send(t)
    emb_i = zbuf[0].astype(f32)
    emb_t = pbuf[0, 0].astype(f32)
    ring_sum(most_up // 2 + 1)
    finish(0, gimg[0], emb_i, emb_t)
    for n in range(1, len(order)):
        arrived(rxy.at[n], xr_sem.at[n - 1])
    total = gtxt[0, 0]
    for n in range(1, len(order)):
        total = total + rxy[n].astype(f32)
    finish(1, total, emb_t, emb_i)
    weight_grad(0)
    over_x(0)
    weight_grad(1)
    over_x(1)
    over_z(0)
    over_z(1)
    collect(0, out_img)
    collect(1, out_txt)
    for copy in sends:
        copy.wait_send()


def on_device(
    pool_img, pool_txt, w_img, w_txt, logit_scale, logit_bias, loss_scale, select, counts
):
    ny = lax.axis_size("tower")
    rows_n = lax.axis_size("rows")
    nz = rows_n // (NX * NC)
    chips = NX * ny
    list_len = select.shape[0]
    slots = list_len // ny
    depth, col_w = w_img.shape
    emb_w = col_w * ny
    out_rows = depth // rows_n
    most_up = nz // 2
    vmem = pltpu.VMEM
    dma = pltpu.SemaphoreType.DMA
    out = jax.ShapeDtypeStruct((out_rows, col_w), f32)
    scratch = [
        vmem((2,) + pool_img.shape, bf16),
        vmem((2, depth, col_w), bf16),
        vmem((list_len,), jnp.int32),
        vmem((2, list_len, depth), bf16),
        vmem((nz, NX, NC, out_rows, list_len), f32),
        vmem((2, NC, depth // NC, list_len), bf16),
        vmem((2, depth // NC, list_len), bf16),
        vmem((2, list_len, col_w), f32),
        vmem((2 * ny, slots, col_w), f32),
        vmem((2, slots, 1), f32),
        vmem((nz, slots, emb_w), bf16),
        vmem((chips, NC, slots, emb_w), bf16),
        vmem((nz, slots, emb_w), f32),
        vmem((chips, NC, slots, emb_w), f32),
        vmem((chips // TILE, (GROUPS[-1] - GROUPS[-2]) * slots, TILE * NC * slots), bf16),
        vmem((nz, slots, emb_w), bf16),
        vmem((most_up, slots, emb_w), bf16),
        vmem((most_up, slots, emb_w), bf16),
        vmem((chips, slots, emb_w), f32),
        vmem((chips, slots, emb_w), bf16),
        vmem((chips, slots, emb_w), bf16),
        vmem((2 * ny, slots, col_w), bf16),
        vmem((2 * NC * ny, slots, col_w), bf16),
        vmem((2, nz, NX, out_rows, col_w), f32),
        vmem((2, nz, NX, out_rows, col_w), f32),
        vmem((2, NX - 1, nz, out_rows, col_w), f32),
        vmem((2, nz, out_rows, col_w), f32),
        vmem((2, nz - 1, out_rows, col_w), f32),
        dma((5,)),
        dma((2, ny - 1, 2)),
        dma((most_up, ZCH, 2)),
        dma((most_up, ZCH, 2)),
        dma((chips - 1, 2)),
        dma((chips, 2)),
        dma((most_up, ZCH, 2)),
        dma((most_up, ZCH, 2)),
        dma((chips // TILE, 2)),
        dma((chips - 1, 2)),
        dma((2, NC, ny, 2)),
        dma((2, 2)),
        dma((2, NX - 1, PARTS, 2)),
        dma((2, nz - 1, 2)),
    ]
    whole = pl.BlockSpec(memory_space=vmem)
    placed = pl.BlockSpec(memory_space=pl.ANY)
    step = pl.pallas_call(
        functools.partial(kernel, (nz, ny)),
        out_shape=(out, out),
        in_specs=[placed] * 5 + [pl.BlockSpec(memory_space=pltpu.SMEM)] * 4,
        out_specs=(whole, whole),
        scratch_shapes=scratch,
        compiler_params=pltpu.CompilerParams(
            collective_id=0, has_side_effects=True, vmem_limit_bytes=60 << 20
        ),
        name="learner_step",
    )(
        pool_img, pool_txt, w_img, w_txt, select, counts,
        logit_scale, logit_bias, loss_scale,
    )
    return pl.pallas_call(
        hand_out, out_shape=(out, out), in_specs=[whole] * 2, out_specs=(whole, whole),
        name="hand_out",
    )(*step)


def hand_out(img, txt, out_img, out_txt):
    out_img[...] = img[...]
    out_txt[...] = txt[...]


def solution(mesh):
    in_specs = (
        P("rows", None),
        P("rows", None),
        P(None, "tower"),
        P(None, "tower"),
        P(),
        P(),
        P(),
        P("rows"),
        P("rows"),
    )
    out_specs = (P("rows", "tower"), P("rows", "tower"))
    return jax.shard_map(
        on_device, mesh=mesh, in_specs=in_specs, out_specs=out_specs, check_vma=False
    )
```
